256 devices in a mesh: dp: 16 (over y_hi, z), feat: 16 (over y_lo, x, core).
Axes of the slice: x: 4, y: 4 (y_hi: 2, y_lo: 2; y = y_hi * 2 + y_lo), z: 8, core: 2. Of those that a mesh axis runs over, the one named last changes fastest.
Arguments:
- x_in: bfloat16 [2048, 4096], P('dp'), may hold values from -6 to 6
- out_grad: bfloat16 [2048, 4096], P('dp'), may hold values from -6 to 6
- gate_tiles: bfloat16 [1792, 128, 128], P(('dp', 'feat')), may hold values from -0.125 to 0.125
- up_tiles: bfloat16 [1792, 128, 128], P(('dp', 'feat')), may hold values from -0.125 to 0.125
- down_tiles: bfloat16 [1792, 128, 128], P(('dp', 'feat')), may hold values from -0.0625 to 0.0625
- gate_spot: int32 [1792], P(('dp', 'feat')), may hold values from -1 to 3583, as said below
- up_spot: int32 [1792], P(('dp', 'feat')), may hold values from -1 to 3583, as said below
- down_spot: int32 [1792], P(('dp', 'feat')), may hold values from -1 to 3583, as said below
Outputs:
- layer_out: bfloat16 [2048, 4096], P('dp', 'feat')
- x_grad: bfloat16 [2048, 4096], P('dp', 'feat')
- gate_grad: bfloat16 [1792, 128, 128], P(('dp', 'feat'))
- up_grad: bfloat16 [1792, 128, 128], P(('dp', 'feat'))
- down_grad: bfloat16 [1792, 128, 128], P(('dp', 'feat'))
The draws below stay inside these ranges and needn't reach their ends.
Inputs may be any that keep to these rules, and one draw needn't show every extreme that they name: `gate_spot`: slot s belongs to device d = s // 7 of dp+feat (dp index d // 16, feat index d % 16). A live gate position lies in block rows dp index * 2 to + 1 and block columns feat index * 7 to + 6; live positions of one device are distinct; -1 marks an empty slot; each device has 1 to 7 live slots, the first device 7, the live ones first. `up_spot`: as for gate_spot, with its own positions and counts. `down_spot`: A live down position has block row in feat index * 7 to + 6 of the hidden units and block column in dp index * 2 to + 1 of the width; otherwise as for gate_spot.
All inputs are finite; a program needn't handle non-finite values.
Results may differ from the reference program's by a relative error of at most 0.028.
Values may be sent and summed in bfloat16 or wider, within the bound.
A program may use at most 128 MiB of HBM per device.

```python
import jax
import jax.numpy as jnp
from jax import lax

D = 4096
FF = 14336
BLK = 128
TOK_DEV = 128
TOKENS = 2048
RB = 2
CB = 7
CAP = 7
SLOTS = 1792
N_DP = 16
N_FEAT = 16


def spot_draw(key, gate_like):
    devices = N_DP * N_FEAT
    places = RB * CB
    keys = jax.random.split(key, devices)
    orders = jax.vmap(lambda one: jax.random.permutation(one, places))(keys)
    final_row = orders[devices - 1]
    shifted = (final_row + (places - 1 - final_row[0])) % places
    orders = orders.at[devices - 1].set(shifted)
    picked = orders[:, :CAP]
    level_key, jitter_key = jax.random.split(jax.random.fold_in(key, 101))
    level = jax.random.randint(level_key, (N_FEAT,), CAP // 2, CAP + 1)
    jitter = jax.random.randint(jitter_key, (devices,), 0, 2)
    count = jnp.maximum(jnp.tile(level, N_DP) - jitter, 1)
    count = count.at[0].set(CAP).at[1].set(max(CAP // 2, 1))
    device = jnp.arange(devices, dtype=jnp.int32)
    first = device // N_FEAT
    second = device % N_FEAT
    if gate_like:
        row = first[:, None] * RB + picked // CB
        col = second[:, None] * CB + picked % CB
        spot = row * (FF // BLK) + col
    else:
        row = second[:, None] * CB + picked // RB
        col = first[:, None] * RB + picked % RB
        spot = row * (D // BLK) + col
    live = jnp.arange(CAP, dtype=jnp.int32)[None, :] < count[:, None]
    return jnp.where(live, spot, -1).reshape(-1).astype(jnp.int32)


def draw_gate_spot(key, part):
    key = jax.random.fold_in(key, 1)
    return spot_draw(key, True)


def draw_up_spot(key, part):
    key = jax.random.fold_in(key, 2)
    return spot_draw(key, True)


def draw_down_spot(key, part):
    key = jax.random.fold_in(key, 3)
    return spot_draw(key, False)


def levels(rng, extent, cuts, least, high):
    loudness = 1.0
    for dim, blocks in cuts:
        draws = jax.random.uniform(jax.random.fold_in(jax.random.fold_in(rng, 6), dim), (blocks,), jnp.float32, least / len(cuts), high / len(cuts))
        loudness = loudness * jnp.repeat(jnp.exp(draws), extent[dim] // blocks).reshape((-1,) + (1,) * (len(extent) - 1 - dim))
    return loudness


def scatter_about(rng, extent, deviation, most, pieces=(), kind=jnp.bfloat16):
    drawn = jax.random.normal(rng, extent, jnp.float32) * deviation
    if len(pieces) > 0:
        drawn = levels(rng, extent, pieces, -0.22, 0.18) * drawn
    return jnp.clip(drawn, min=-most, max=most).astype(kind)


def setup_inputs(seed: int = 0) -> dict:
    key_of = jax.random.split(jax.random.key(seed), 9)
    return {
        "x_in": scatter_about(key_of[0], (TOKENS, D), 1.0, 6.0, ((0, 16),)),
        "out_grad": scatter_about(key_of[1], (TOKENS, D), 1.0, 6.0, ((0, 16),)),
        "gate_tiles": scatter_about(key_of[2], (SLOTS, BLK, BLK), (D // 2) ** -0.5, 0.125, ((0, 256),)),
        "up_tiles": scatter_about(key_of[3], (SLOTS, BLK, BLK), (D // 2) ** -0.5, 0.125, ((0, 256),)),
        "down_tiles": scatter_about(key_of[4], (SLOTS, BLK, BLK), (FF // 2) ** -0.5, 0.0625, ((0, 256),)),
        "gate_spot": draw_gate_spot(jax.random.fold_in(key_of[8], 71), 0),
        "up_spot": draw_up_spot(jax.random.fold_in(key_of[8], 71), 0),
        "down_spot": draw_down_spot(jax.random.fold_in(key_of[8], 71), 0),
    }


def dense_from(tiles, spots, row_blocks, col_blocks):
    live = spots >= 0
    safe = jnp.maximum(spots, 0)
    rows = safe // col_blocks
    cols = safe % col_blocks
    kept = tiles * live[:, None, None].astype(tiles.dtype)
    grid = jnp.zeros((row_blocks, col_blocks, BLK, BLK), tiles.dtype).at[rows, cols].add(kept)
    return grid.transpose(0, 2, 1, 3).reshape(row_blocks * BLK, col_blocks * BLK)


def rounded(value):
    return lax.optimization_barrier(value.astype(jnp.bfloat16)).astype(jnp.float32)


def slot_terms(left, right, spots, col_blocks, left_blocks, right_blocks):
    live = spots >= 0
    safe = jnp.maximum(spots, 0)
    rows = safe // col_blocks
    cols = safe % col_blocks
    left_part = left.reshape(left.shape[0], left_blocks, BLK)[:, rows]
    right_part = right.reshape(right.shape[0], right_blocks, BLK)[:, cols]
    term = jnp.einsum("tsk,tsn->skn", left_part.astype(jnp.float32), right_part.astype(jnp.float32))
    return term * live[:, None, None].astype(jnp.float32)


def reference(x_in, out_grad, gate_tiles, up_tiles, down_tiles, gate_spot, up_spot, down_spot):
    dblocks = D // BLK
    fblocks = FF // BLK
    wg = dense_from(gate_tiles, gate_spot, dblocks, fblocks)
    wu = dense_from(up_tiles, up_spot, dblocks, fblocks)
    wd = dense_from(down_tiles, down_spot, fblocks, dblocks)
    gate = jnp.dot(x_in, wg, preferred_element_type=jnp.float32)
    up = jnp.dot(x_in, wu, preferred_element_type=jnp.float32)
    hidden = (jax.nn.silu(gate) * up).astype(jnp.bfloat16)
    group = FF // N_FEAT

    def out_step(total, index):
        start = (index * group).astype(jnp.int32)
        hid = lax.dynamic_slice_in_dim(hidden, start, group, 1)
        wpart = lax.dynamic_slice_in_dim(wd, start, group, 0)
        return total + rounded(jnp.dot(hid, wpart, preferred_element_type=jnp.float32)), None

    groups = jnp.arange(N_FEAT, dtype=jnp.int32)
    total, _ = lax.scan(out_step, jnp.zeros((TOKENS, D), jnp.float32), groups)
    layer_out = total.astype(jnp.bfloat16)
    dh = jnp.dot(out_grad, wd.T, preferred_element_type=jnp.float32)
    sig = jax.nn.sigmoid(gate)
    dgate = (dh * up * sig * (1.0 + gate * (1.0 - sig))).astype(jnp.bfloat16)
    dup = (dh * gate * sig).astype(jnp.bfloat16)

    def back_step(total, index):
        start = (index * group).astype(jnp.int32)
        dg = lax.dynamic_slice_in_dim(dgate, start, group, 1)
        du = lax.dynamic_slice_in_dim(dup, start, group, 1)
        gpart = lax.dynamic_slice_in_dim(wg, start, group, 1)
        upart = lax.dynamic_slice_in_dim(wu, start, group, 1)
        part = jnp.dot(dg, gpart.T, preferred_element_type=jnp.float32) + jnp.dot(du, upart.T, preferred_element_type=jnp.float32)
        return total + rounded(part), None

    total, _ = lax.scan(back_step, jnp.zeros((TOKENS, D), jnp.float32), groups)
    x_grad = total.astype(jnp.bfloat16)

    def grad_step(totals, index):
        start = (index * TOK_DEV).astype(jnp.int32)
        xs = lax.dynamic_slice_in_dim(x_in, start, TOK_DEV, 0)
        dgs = lax.dynamic_slice_in_dim(dgate, start, TOK_DEV, 0)
        dus = lax.dynamic_slice_in_dim(dup, start, TOK_DEV, 0)
        hs = lax.dynamic_slice_in_dim(hidden, start, TOK_DEV, 0)
        dys = lax.dynamic_slice_in_dim(out_grad, start, TOK_DEV, 0)
        gate_term = rounded(slot_terms(xs, dgs, gate_spot, fblocks, dblocks, fblocks))
        up_term = rounded(slot_terms(xs, dus, up_spot, fblocks, dblocks, fblocks))
        down_term = rounded(slot_terms(hs, dys, down_spot, dblocks, fblocks, dblocks))
        return (totals[0] + gate_term, totals[1] + up_term, totals[2] + down_term), None

    empty = jnp.zeros((SLOTS, BLK, BLK), jnp.float32)
    sums, _ = lax.scan(grad_step, (empty, empty, empty), jnp.arange(N_DP, dtype=jnp.int32))
    return (layer_out, x_grad, sums[0].astype(jnp.bfloat16), sums[1].astype(jnp.bfloat16), sums[2].astype(jnp.bfloat16))
```

```python
import jax
import jax.numpy as jnp
from jax import lax
from jax.experimental import pallas as pl
from jax.experimental.pallas import tpu as pltpu
from jax.sharding import PartitionSpec as P

BF, F32 = jnp.bfloat16, jnp.float32
B = 128
NZ = 8
CUT = ((0, 4), (4, 7))
MESH = pl.DeviceIdType.MESH


def dot(a, b):
    return lax.dot_general(a, b, (((1,), (0,)), ((), ())), preferred_element_type=F32)


def dot_nt(a, b):
    return lax.dot_general(a, b, (((1,), (1,)), ((), ())), preferred_element_type=F32)


def role(m, d):
    return (d + (1 if m == 1 else 0)) % 2


def kernel(
    x_ref, dy_ref, gt, ut, dt, gs, us, ds,
    o_out, o_xg, o_gg, o_ug, o_dg,
    tabv, tabs, xk, dyk, xt, ht, stage, wb, wg, wu, wd, acc, ps, pr, hid, dg, du, grid,
    rss, rsr, ost, r1, s1, r2, s2f, s2b, r3, s3, r4,
    tab_ss, tab_rs, tab_ls, x_ss, x_rs, ag_ss, ag_rs, y_ss, y_rs, rs_ss, rs_rs,
    c_ss, c_rs, f_ss, f_rs, l_ss, l_rs, d_ss, d_rs,
):
    dp, ft = lax.axis_index("dp"), lax.axis_index("feat")
    yh, z = dp // 8, lax.rem(dp, 8)
    yl, xx, core = ft // 8, lax.rem(ft // 2, 4), lax.rem(ft, 2)

    def at_z(n):
        return lax.rem(z + (n % NZ), NZ)

    zdev = [(yh * 8 + at_z(1), ft), (yh * 8 + at_z(-1), ft)]
    zall = [(yh * 8 + at_z(n), ft) for n in range(1, NZ)]
    ydev = ((1 - yh) * 8 + z, ft)
    cdev = (dp, yl * 8 + xx * 2 + (1 - core))
    xdev = [(dp, yl * 8 + lax.rem(xx + n, 4) * 2 + core) for n in (1, 2, 3)]
    ldev = (dp, (1 - yl) * 8 + xx * 2 + core)
    ddev = ((1 - yh) * 8 + z, (1 - yl) * 8 + xx * 2 + core)

    barrier = pltpu.get_barrier_semaphore()
    peers = zall + [ydev, cdev] + xdev + [ldev, ddev]
    for dev in peers:
        pl.semaphore_signal(barrier, inc=1, device_id=dev, device_id_type=MESH)

    lane = lax.broadcasted_iota(jnp.int32, (8, B), 1)
    seg, q = lane >> 5, lane & 31
    tab = jnp.where(q < 14, 7, 14)
    for m, spots in enumerate((gs, us, ds)):
        for s in range(7):
            spot = spots[s]
            safe = jnp.maximum(spot, 0)
            if m < 2:
                place = (lax.div(safe, 112) - 2 * dp) * 7 + lax.rem(safe, 112) - 7 * ft
            else:
                place = (lax.div(safe, 32) - 7 * ft) * 2 + lax.rem(safe, 32) - 2 * dp
            place = jnp.where(spot >= 0, jnp.clip(place, 0, 13), 14)
            tab = jnp.where((seg == m) & (q < 14) & (q == place), s, tab)
            tab = jnp.where((seg == m) & (q == 16 + s), place, tab)
    tabv[z] = tab

    pl.semaphore_wait(barrier, len(peers))

    def rc(src, dst, ss, rs, dev):
        return pltpu.make_async_remote_copy(
            src_ref=src, dst_ref=dst, send_sem=ss, recv_sem=rs, device_id=dev, device_id_type=MESH
        )

    sent = []

    def go(copy):
        copy.start()
        sent.append(copy)

    own = (gt, ut, dt)
    w = (wg, wu, wd)

    def piece(p):
        return pl.ds(CUT[p][0], CUT[p][1] - CUT[p][0])

    def ag_send(m, d, s, p):
        o = at_z(-s if d == 0 else s)
        src = own[m].at[piece(p)] if s == 0 else wb.at[m, o, piece(p)]
        go(rc(src, wb.at[m, o, piece(p)], ag_ss.at[m, d, s, p], ag_rs.at[m, d, s, p], zdev[d]))

    def ag_arrive(m, d, s, p):
        o = at_z(-s - 1 if d == 0 else s + 1)
        here = wb.at[m, o, piece(p)]
        rc(here, here, ag_ss.at[m, d, s, p], ag_rs.at[m, d, s, p], zdev[d]).wait_recv()

    def ag_first(m):
        for p in range(2):
            for d in range(2):
                ag_send(m, d, 0, p)

    for i, dev in enumerate(zall):
        go(rc(tabv.at[z], tabv.at[z], tab_ss.at[i], tab_rs.at[i], dev))
    ag_first(0)
    order = (0, -1, 1, -2, 2, -3, 3, 4)
    for a, (src, dst) in enumerate(((x_ref, xk), (dy_ref, dyk))):
        for n in order:
            k = at_z(n)
            cols = pl.ds(pl.multiple_of(((1 - yh) * 8 + k) * 256, 256), 256)
            go(rc(src.at[:, cols], dst.at[k, pl.ds(B, B)], x_ss.at[a, k], x_rs.at[a, k], ydev))

    @pl.loop(0, NZ)
    def _(k):
        cols = pl.ds(pl.multiple_of((yh * 8 + k) * 256, 256), 256)
        xk[k, 0:B] = x_ref[:, cols]
        dyk[k, 0:B] = dy_ref[:, cols]

    stage[7] = jnp.zeros((B, B), BF)
    grid[0, 14] = jnp.zeros((B, B), F32)
    grid[1, 14] = jnp.zeros((B, B), F32)
    grid[2, 14] = jnp.zeros((B, B), F32)

    for i, n in enumerate(range(1, NZ)):
        here = tabv.at[at_z(-n)]
        rc(here, here, tab_ss.at[i], tab_rs.at[i], zall[i]).wait_recv()
    tabcopy = pltpu.make_async_copy(tabv, tabs, tab_ls)
    tabcopy.start()
    tabcopy.wait()

    def x_arrive(a, k):
        dst = (xk, dyk)[a]
        here = dst.at[k, pl.ds(B, B)]
        rc(here, here, x_ss.at[a, k], x_rs.at[a, k], ydev).wait_recv()

    def block(m, o, first=False, last=False):
        if m == 0:
            x_arrive(0, o)
        if m == 2 and not last:
            x_arrive(1, o)
        stage[0:7] = own[m][...] if first else wb[m, o]
        cols = 7 if m < 2 else 2
        for p in range(14):
            r, c = divmod(p, cols)
            w[m][o, r * B : (r + 1) * B, c * B : (c + 1) * B] = stage[tabs[o, 0, m * 32 + p]]
        if m == 1:
            xt[o] = xk[o].T
        term = dot(xk[o], w[m][o]) if m < 2 else dot_nt(dyk[o], wd[o])
        if first:
            acc[m] = term
        else:
            acc[m] += term

    def pair(m, s):
        @pl.loop(0, 2)
        def _(d):
            block(m, lax.rem(z + NZ + (2 * d - 1) * (s + 1), NZ))

    def ag_step(m, s):
        for p in range(2):
            for d in range(2):
                if s == 3 and p != role(m, d):
                    continue
                ag_arrive(m, d, s, p)
                if s < 2 or (s == 2 and p == role(m, d)):
                    ag_send(m, d, s + 1, p)

    def y_copy(m):
        return rc(ps.at[m], pr.at[m], y_ss.at[m], y_rs.at[m], ydev)

    def exchange(m):
        ps[m] = acc[m].astype(BF)
        go(y_copy(m))

    def halves(m, i):
        rows = pl.ds(pl.multiple_of(i * 16, 16), 16)
        rest = pl.ds(pl.multiple_of(i * 16 + B, 16), 16)
        return (
            (rows, acc[m, rows] + pr[m, rest].astype(F32)),
            (rest, acc[m, rest] + pr[m, rows].astype(F32)),
        )

    def make_hidden():
        y_copy(0).wait_recv()
        y_copy(1).wait_recv()

        @pl.loop(0, 8)
        def _(i):
            for (rows, g), (_, u) in zip(halves(0, i), halves(1, i)):
                sig = jax.nn.sigmoid(g)
                silu = g * sig
                hid[rows] = (silu * u).astype(BF)
                acc[0, rows] = u * sig * (1.0 + g * (1.0 - sig))
                acc[1, rows] = silu

        for i in range(7):
            ht[i * B : (i + 1) * B] = hid[:, i * B : (i + 1) * B].T

    def make_grads():
        y_copy(2).wait_recv()

        @pl.loop(0, 8)
        def _(i):
            for rows, dh in halves(2, i):
                dg[rows] = (dh * acc[0, rows]).astype(BF)
                du[rows] = (dh * acc[1, rows]).astype(BF)

    def grad_grid(m, k, i):
        if m == 2:
            term = dot(ht[...], dyk[k])
        else:
            term = dot(xt[k], (dg, du)[m][...])
        cols = 7 if m < 2 else 2
        for p in range(14):
            r, c = divmod(p, cols)
            grid[i, p] = term[r * B : (r + 1) * B, c * B : (c + 1) * B]

    def rs_copy(m, d, s, p):
        part = piece(p)
        return rc(
            rss.at[m, d, s, part], rsr.at[m, d, s, part],
            rs_ss.at[m, d, s, p], rs_rs.at[m, d, s, p], zdev[d],
        )

    def rs_send(m, d, s, p, k, i):
        add = s >= 2 or (s == 1 and p == role(m, d))
        if add:
            rs_copy(m, d, s - 1, p).wait_recv()
        for t in range(*CUT[p]):
            v = grid[i, tabs[k, 0, m * 32 + 16 + t]]
            if add:
                v = v + rsr[m, d, s - 1, t].astype(F32)
            rss[m, d, s, t] = v.astype(BF)
        go(rs_copy(m, d, s, p))

    def rs_a(m, s):
        if s == 0:
            k = at_z(4)
            grad_grid(m, k, 0)
            for d in range(2):
                rs_send(m, d, 0, role(m, d), k, 0)
            return
        for d in range(2):
            k = at_z(4 - s if d == 0 else 4 + s)
            grad_grid(m, k, d)
        for d in range(2):
            k = at_z(4 - s if d == 0 else 4 + s)
            rs_send(m, d, s, 1 - role(m, d), k, d)

    def rs_b(m, s):
        for d in range(2):
            k = at_z(4 - s if d == 0 else 4 + s)
            rs_send(m, d, s, role(m, d), k, d)

    def rs(m, s):
        rs_a(m, s)
        rs_b(m, s)

    def rs_last(m):
        grad_grid(m, z, 2)
        for p in range(2):
            for d in range(2):
                rs_copy(m, d, 3, p).wait_recv()
        for t in range(7):
            v = grid[2, tabs[z, 0, m * 32 + 16 + t]]
            v = v + rsr[m, 0, 3, t].astype(F32) + rsr[m, 1, 3, t].astype(F32)
            (o_gg, o_ug, o_dg)[m][t] = v.astype(BF)

    def partial(a, cc):
        @pl.loop(0, 4)
        def _(cx):
            k = 2 * cx + cc
            if a == 0:
                term = dot(hid[...], wd[k])
            else:
                term = dot_nt(dg[...], wg[k]) + dot_nt(du[...], wu[k])
            ost[a, cc, cx] = term.astype(BF)

    def c_copy(a):
        return rc(ost.at[a, 1 - core], r1.at[a], c_ss.at[a], c_rs.at[a], cdev)

    def f_copy(a, n):
        cx = lax.rem(xx + n, 4)
        return rc(s1.at[a, cx], r2.at[a, n - 1], f_ss.at[a, n - 1], f_rs.at[a, n - 1], xdev[n - 1])

    def l_copy(a):
        return rc(s2b.at[a], r3.at[a], l_ss.at[a], l_rs.at[a], ldev)

    def d_copy(a):
        return rc(s3.at[a], r4.at[a], d_ss.at[a], d_rs.at[a], ddev)

    def over_cores(a):
        partial(a, 1 - core)
        go(c_copy(a))

    def over_x(a):
        c_copy(a).wait_recv()
        for n in (2, 1, 3):
            cx = lax.rem(xx + n, 4)
            s1[a, cx] = (ost[a, core, cx].astype(F32) + r1[a, cx].astype(F32)).astype(BF)
            go(f_copy(a, n))

    give = lax.rem(yh + 1 - yl, 2)

    def over_yl(a):
        for n in (1, 2, 3):
            f_copy(a, n).wait_recv()
        for h in range(2):
            rows = slice(h * B, (h + 1) * B)
            v = ost[a, core, xx, rows].astype(F32) + r1[a, xx, rows].astype(F32)
            for n in range(3):
                v = v + r2[a, n, rows].astype(F32)
            s2f[h] = v
        s2b[a] = s2f[give].astype(BF)
        go(l_copy(a))
        s2f[2 + a] = s2f[1 - give]

    def to_owner(a):
        l_copy(a).wait_recv()
        s3[a] = (s2f[2 + a] + r3[a].astype(F32)).astype(BF)

        @pl.when(yh != yl)
        def _():
            d_copy(a).start()

    def out_last(a):
        o = (o_out, o_xg)[a]

        @pl.when(yh != yl)
        def _():
            d_copy(a).wait()
            o[...] = r4[a]

        @pl.when(yh == yl)
        def _():
            o[...] = s3[a]

    for m in range(3):
        block(m, z, first=True)
        for s in range(4):
            if m == 2 and s == 3:
                make_hidden()
                x_arrive(1, at_z(4))
                rs_a(2, 0)
                rs_a(2, 1)
            ag_step(m, s)
            if s == 2 and m < 2:
                ag_first(m + 1)
            if s < 3:
                pair(m, s)
            else:
                block(m, at_z(4), last=True)
        exchange(m)

    over_cores(0)
    rs_b(2, 1)
    partial(0, core)
    rs(2, 2)
    over_x(0)
    rs(2, 3)
    make_grads()
    rs_a(0, 0)
    rs_a(0, 1)
    rs_last(2)
    over_cores(1)
    rs_b(0, 1)
    partial(1, core)
    rs(0, 2)
    over_x(1)
    over_yl(0)
    rs(0, 3)
    rs_a(1, 0)
    rs_a(1, 1)
    rs_last(0)
    to_owner(0)
    rs_b(1, 1)
    over_yl(1)
    rs(1, 2)
    out_last(0)
    to_owner(1)
    rs(1, 3)
    out_last(1)
    rs_last(1)
    for copy in sent:
        copy.wait_send()


def on_device(x_in, out_grad, gate_tiles, up_tiles, down_tiles, gate_spot, up_spot, down_spot):
    vmem = pl.BlockSpec(memory_space=pltpu.VMEM)
    smem = pl.BlockSpec(memory_space=pltpu.SMEM)
    dma = pltpu.SemaphoreType.DMA
    tile = jax.ShapeDtypeStruct((7, B, B), BF)
    act = jax.ShapeDtypeStruct((B, 256), BF)
    scratch = [
        pltpu.VMEM((NZ, 8, B), jnp.int32),
        pltpu.SMEM((NZ, 8, B), jnp.int32),
        pltpu.VMEM((NZ, 256, 256), BF),
        pltpu.VMEM((NZ, 256, 256), BF),
        pltpu.VMEM((NZ, 256, 256), BF),
        pltpu.VMEM((896, 256), BF),
        pltpu.VMEM((8, B, B), BF),
        pltpu.VMEM((3, NZ, 7, B, B), BF),
        pltpu.VMEM((NZ, 256, 896), BF),
        pltpu.VMEM((NZ, 256, 896), BF),
        pltpu.VMEM((NZ, 896, 256), BF),
        pltpu.VMEM((3, 256, 896), F32),
        pltpu.VMEM((3, 256, 896), BF),
        pltpu.VMEM((3, 256, 896), BF),
        pltpu.VMEM((256, 896), BF),
        pltpu.VMEM((256, 896), BF),
        pltpu.VMEM((256, 896), BF),
        pltpu.VMEM((3, 15, B, B), F32),
        pltpu.VMEM((3, 2, 4, 7, B, B), BF),
        pltpu.VMEM((3, 2, 4, 7, B, B), BF),
        pltpu.VMEM((2, 2, 4, 256, 256), BF),
        pltpu.VMEM((2, 4, 256, 256), BF),
        pltpu.VMEM((2, 4, 256, 256), BF),
        pltpu.VMEM((2, 3, 256, 256), BF),
        pltpu.VMEM((4, B, 256), F32),
        pltpu.VMEM((2, B, 256), BF),
        pltpu.VMEM((2, B, 256), BF),
        pltpu.VMEM((2, B, 256), BF),
        pltpu.VMEM((2, B, 256), BF),
        dma((7,)), dma((7,)), dma,
        dma((2, NZ)), dma((2, NZ)),
        dma((3, 2, 4, 2)), dma((3, 2, 4, 2)),
        dma((3,)), dma((3,)),
        dma((3, 2, 4, 2)), dma((3, 2, 4, 2)),
        dma((2,)), dma((2,)),
        dma((2, 3)), dma((2, 3)),
        dma((2,)), dma((2,)),
        dma((2,)), dma((2,)),
    ]
    return pl.pallas_call(
        kernel,
        out_shape=(act, act, tile, tile, tile),
        in_specs=[vmem] * 5 + [smem] * 3,
        out_specs=(vmem,) * 5,
        scratch_shapes=scratch,
        compiler_params=pltpu.CompilerParams(
            collective_id=0, has_side_effects=True, vmem_limit_bytes=60 * 2**20
        ),
        cost_estimate=pl.CostEstimate(flops=8_500_000_000, bytes_accessed=6_000_000, transcendentals=229_376),
        name="layer",
    )(x_in, out_grad, gate_tiles, up_tiles, down_tiles, gate_spot, up_spot, down_spot)


def solution(mesh):
    blocks, spots = P(("dp", "feat"), None, None), P(("dp", "feat"))
    return jax.shard_map(
        on_device,
        mesh=mesh,
        in_specs=(P("dp", None),) * 2 + (blocks,) * 3 + (spots,) * 3,
        out_specs=(P("dp", "feat"),) * 2 + (blocks,) * 3,
        check_vma=False,
    )
```

```python
import jax
import jax.numpy as jnp
from jax import lax
from jax.experimental import pallas as pl
from jax.experimental.pallas import tpu as pltpu
from jax.sharding import PartitionSpec as P

BF, F32 = jnp.bfloat16, jnp.float32
B = 128
NZ = 8
CUT = ((0, 4), (4, 7))
MESH = pl.DeviceIdType.MESH


def dot(a, b):
    return lax.dot_general(a, b, (((1,), (0,)), ((), ())), preferred_element_type=F32)


def dot_nt(a, b):
    return lax.dot_general(a, b, (((1,), (1,)), ((), ())), preferred_element_type=F32)


def role(m, d):
    return (d + (1 if m == 1 else 0)) % 2


def kernel(
    x_ref, dy_ref, gt, ut, dt, gs, us, ds,
    o_act, o_grad,
    tabv, tabs, xk, dyk, xt, ht, stage, wb, wg, wu, wd, acc, ps, pr, hid, dg, du, grid,
    rss, rsr, ost, r1, s1, r2, s2f, s2b, r3, s3, r4,
    tab_ss, tab_rs, tab_ls, in_ls, w_ls, x_ss, x_rs, ag_ss, ag_rs, y_ss, y_rs, rs_ss, rs_rs,
    c_ss, c_rs, f_ss, f_rs, l_ss, l_rs, d_ss, d_rs,
):
    dp, ft = lax.axis_index("dp"), lax.axis_index("feat")
    yh, z = dp // 8, lax.rem(dp, 8)
    yl, xx, core = ft // 8, lax.rem(ft // 2, 4), lax.rem(ft, 2)

    def at_z(n):
        return lax.rem(z + (n % NZ), NZ)

    zdev = [(yh * 8 + at_z(1), ft), (yh * 8 + at_z(-1), ft)]
    zall = [(yh * 8 + at_z(n), ft) for n in range(1, NZ)]
    ydev = ((1 - yh) * 8 + z, ft)
    cdev = (dp, yl * 8 + xx * 2 + (1 - core))
    xdev = [(dp, yl * 8 + lax.rem(xx + n, 4) * 2 + core) for n in (1, 2, 3)]
    ldev = (dp, (1 - yl) * 8 + xx * 2 + core)
    ddev = ((1 - yh) * 8 + z, (1 - yl) * 8 + xx * 2 + core)

    barrier = pltpu.get_barrier_semaphore()
    peers = zall + [ydev, cdev] + xdev + [ldev, ddev]
    for dev in peers:
        pl.semaphore_signal(barrier, inc=1, device_id=dev, device_id_type=MESH)

    own = (gt, ut, dt)

    def in_copy(a, k):
        cols = pl.ds(pl.multiple_of((yh * 8 + k) * 256, 256), 256)
        return pltpu.make_async_copy((x_ref, dy_ref)[a].at[:, cols], (xk, dyk)[a].at[k, pl.ds(0, B)], in_ls.at[a, k])

    def w_copy(m):
        return pltpu.make_async_copy(own[m], wb.at[m, z], w_ls.at[m])

    for m in range(3):
        w_copy(m).start()
    for a in range(2):
        for k in range(NZ):
            in_copy(a, k).start()

    lane = lax.broadcasted_iota(jnp.int32, (8, B), 1)
    seg, q = lane >> 5, lane & 31
    tab = jnp.where(q < 14, 7, 14)
    for m, spots in enumerate((gs, us, ds)):
        for s in range(7):
            spot = spots[s]
            safe = jnp.maximum(spot, 0)
            if m < 2:
                place = (lax.div(safe, 112) - 2 * dp) * 7 + lax.rem(safe, 112) - 7 * ft
            else:
                place = (lax.div(safe, 32) - 7 * ft) * 2 + lax.rem(safe, 32) - 2 * dp
            place = jnp.where(spot >= 0, jnp.clip(place, 0, 13), 14)
            tab = jnp.where((seg == m) & (q < 14) & (q == place), s, tab)
            tab = jnp.where((seg == m) & (q == 16 + s), place, tab)
    tabv[z] = tab

    pl.semaphore_wait(barrier, len(peers))

    def rc(src, dst, ss, rs, dev):
        return pltpu.make_async_remote_copy(
            src_ref=src, dst_ref=dst, send_sem=ss, recv_sem=rs, device_id=dev, device_id_type=MESH
        )

    sent = []

    def go(copy):
        copy.start()
        sent.append(copy)

    w = (wg, wu, wd)

    def piece(p):
        return pl.ds(CUT[p][0], CUT[p][1] - CUT[p][0])

    def ag_send(m, d, s, p):
        o = at_z(-s if d == 0 else s)
        src = own[m].at[piece(p)] if s == 0 else wb.at[m, o, piece(p)]
        go(rc(src, wb.at[m, o, piece(p)], ag_ss.at[m, d, s, p], ag_rs.at[m, d, s, p], zdev[d]))

    def ag_arrive(m, d, s, p):
        o = at_z(-s - 1 if d == 0 else s + 1)
        here = wb.at[m, o, piece(p)]
        rc(here, here, ag_ss.at[m, d, s, p], ag_rs.at[m, d, s, p], zdev[d]).wait_recv()

    def ag_first(m):
        for p in range(2):
            for d in range(2):
                ag_send(m, d, 0, p)

    for i, dev in enumerate(zall):
        go(rc(tabv.at[z], tabv.at[z], tab_ss.at[i], tab_rs.at[i], dev))
    ag_first(0)
    order = (0, -1, 1, -2, 2, -3, 3, 4)
    for a, (src, dst) in enumerate(((x_ref, xk), (dy_ref, dyk))):
        for n in order:
            k = at_z(n)
            cols = pl.ds(pl.multiple_of(((1 - yh) * 8 + k) * 256, 256), 256)
            go(rc(src.at[:, cols], dst.at[k, pl.ds(B, B)], x_ss.at[a, k], x_rs.at[a, k], ydev))

    stage[7] = jnp.zeros((B, B), BF)
    grid[0, 14] = jnp.zeros((B, B), F32)
    grid[1, 14] = jnp.zeros((B, B), F32)
    grid[2, 14] = jnp.zeros((B, B), F32)

    for i, n in enumerate(range(1, NZ)):
        here = tabv.at[at_z(-n)]
        rc(here, here, tab_ss.at[i], tab_rs.at[i], zall[i]).wait_recv()
    tabcopy = pltpu.make_async_copy(tabv, tabs, tab_ls)
    tabcopy.start()

    def x_arrive(a, k):
        dst = (xk, dyk)[a]
        here = dst.at[k, pl.ds(B, B)]
        in_copy(a, k).wait()
        rc(here, here, x_ss.at[a, k], x_rs.at[a, k], ydev).wait_recv()

    def block(m, o, first=False, last=False):
        if m == 0:
            x_arrive(0, o)
        if m == 2 and not last:
            x_arrive(1, o)
        if first:
            w_copy(m).wait()
        stage[0:7] = wb[m, o]
        cols = 7 if m < 2 else 2
        for p in range(14):
            r, c = divmod(p, cols)
            w[m][o, r * B : (r + 1) * B, c * B : (c + 1) * B] = stage[tabs[o, 0, m * 32 + p]]
        if m == 1:
            xt[o] = xk[o].T
        term = dot(xk[o], w[m][o]) if m < 2 else dot_nt(dyk[o], wd[o])
        if first:
            acc[m] = term
        else:
            acc[m] += term

    def pair(m, s):
        @pl.loop(0, 2)
        def _(d):
            block(m, lax.rem(z + NZ + (2 * d - 1) * (s + 1), NZ))

    def ag_step(m, s):
        for p in range(2):
            for d in range(2):
                if s == 3 and p != role(m, d):
                    continue
                ag_arrive(m, d, s, p)
                if s < 2 or (s == 2 and p == role(m, d)):
                    ag_send(m, d, s + 1, p)

    def y_copy(m):
        return rc(ps.at[m], pr.at[m], y_ss.at[m], y_rs.at[m], ydev)

    def exchange(m):
        ps[m] = acc[m].astype(BF)
        go(y_copy(m))

    def halves(m, i):
        rows = pl.ds(pl.multiple_of(i * 16, 16), 16)
        rest = pl.ds(pl.multiple_of(i * 16 + B, 16), 16)
        return (
            (rows, acc[m, rows] + pr[m, rest].astype(F32)),
            (rest, acc[m, rest] + pr[m, rows].astype(F32)),
        )

    def make_hidden():
        y_copy(0).wait_recv()
        y_copy(1).wait_recv()

        @pl.loop(0, 8)
        def _(i):
            for (rows, g), (_, u) in zip(halves(0, i), halves(1, i)):
                sig = jax.nn.sigmoid(g)
                silu = g * sig
                hid[rows] = (silu * u).astype(BF)
                acc[0, rows] = u * sig * (1.0 + g * (1.0 - sig))
                acc[1, rows] = silu

        for i in range(7):
            ht[i * B : (i + 1) * B] = hid[:, i * B : (i + 1) * B].T

    def make_grads():
        y_copy(2).wait_recv()

        @pl.loop(0, 8)
        def _(i):
            for rows, dh in halves(2, i):
                dg[rows] = (dh * acc[0, rows]).astype(BF)
                du[rows] = (dh * acc[1, rows]).astype(BF)

    def grad_grid(m, k, i):
        if m == 2:
            term = dot(ht[...], dyk[k])
        else:
            term = dot(xt[k], (dg, du)[m][...])
        cols = 7 if m < 2 else 2
        for p in range(14):
            r, c = divmod(p, cols)
            grid[i, p] = term[r * B : (r + 1) * B, c * B : (c + 1) * B]

    def rs_copy(m, d, s, p):
        part = piece(p)
        return rc(
            rss.at[m, d, s, part], rsr.at[m, d, s, part],
            rs_ss.at[m, d, s, p], rs_rs.at[m, d, s, p], zdev[d],
        )

    def rs_send(m, d, s, p, k, i):
        add = s >= 2 or (s == 1 and p == role(m, d))
        if add:
            rs_copy(m, d, s - 1, p).wait_recv()
        for t in range(*CUT[p]):
            v = grid[i, tabs[k, 0, m * 32 + 16 + t]]
            if add:
                v = v + rsr[m, d, s - 1, t].astype(F32)
            rss[m, d, s, t] = v.astype(BF)
        go(rs_copy(m, d, s, p))

    def rs_a(m, s):
        if s == 0:
            k = at_z(4)
            grad_grid(m, k, 0)
            for d in range(2):
                rs_send(m, d, 0, role(m, d), k, 0)
            return
        for d in range(2):
            k = at_z(4 - s if d == 0 else 4 + s)
            grad_grid(m, k, d)
        for d in range(2):
            k = at_z(4 - s if d == 0 else 4 + s)
            rs_send(m, d, s, 1 - role(m, d), k, d)

    def rs_b(m, s):
        for d in range(2):
            k = at_z(4 - s if d == 0 else 4 + s)
            rs_send(m, d, s, role(m, d), k, d)

    def rs(m, s):
        rs_a(m, s)
        rs_b(m, s)

    def rs_last(m):
        grad_grid(m, z, 2)
        for p in range(2):
            for d in range(2):
                rs_copy(m, d, 3, p).wait_recv()
        for t in range(7):
            v = grid[2, tabs[z, 0, m * 32 + 16 + t]]
            v = v + rsr[m, 0, 3, t].astype(F32) + rsr[m, 1, 3, t].astype(F32)
            o_grad[m * 7 + t] = v.astype(BF)

    def partial(a, cc):
        @pl.loop(0, 4)
        def _(cx):
            k = 2 * cx + cc
            if a == 0:
                term = dot(hid[...], wd[k])
            else:
                term = dot_nt(dg[...], wg[k]) + dot_nt(du[...], wu[k])
            ost[a, cc, cx] = term.astype(BF)

    def c_copy(a):
        return rc(ost.at[a, 1 - core], r1.at[a], c_ss.at[a], c_rs.at[a], cdev)

    def f_copy(a, n):
        cx = lax.rem(xx + n, 4)
        return rc(s1.at[a, cx], r2.at[a, n - 1], f_ss.at[a, n - 1], f_rs.at[a, n - 1], xdev[n - 1])

    def l_copy(a):
        return rc(s2b.at[a], r3.at[a], l_ss.at[a], l_rs.at[a], ldev)

    def d_copy(a):
        return rc(s3.at[a], r4.at[a], d_ss.at[a], d_rs.at[a], ddev)

    def over_cores(a):
        partial(a, 1 - core)
        go(c_copy(a))

    def over_x(a):
        c_copy(a).wait_recv()
        for n in (2, 1, 3):
            cx = lax.rem(xx + n, 4)
            s1[a, cx] = (ost[a, core, cx].astype(F32) + r1[a, cx].astype(F32)).astype(BF)
            go(f_copy(a, n))

    give = lax.rem(yh + 1 - yl, 2)

    def over_yl(a):
        for n in (1, 2, 3):
            f_copy(a, n).wait_recv()
        for h in range(2):
            rows = slice(h * B, (h + 1) * B)
            v = ost[a, core, xx, rows].astype(F32) + r1[a, xx, rows].astype(F32)
            for n in range(3):
                v = v + r2[a, n, rows].astype(F32)
            s2f[h] = v
        s2b[a] = s2f[give].astype(BF)
        go(l_copy(a))
        s2f[2 + a] = s2f[1 - give]

    def to_owner(a):
        l_copy(a).wait_recv()
        s3[a] = (s2f[2 + a] + r3[a].astype(F32)).astype(BF)

        @pl.when(yh != yl)
        def _():
            d_copy(a).start()

    def out_last(a):
        @pl.when(yh != yl)
        def _():
            d_copy(a).wait()
            o_act[a] = r4[a]

        @pl.when(yh == yl)
        def _():
            o_act[a] = s3[a]

    ag_step(0, 0)
    tabcopy.wait()
    for m in range(3):
        block(m, z, first=True)
        for s in range(4):
            if m == 2 and s == 3:
                make_hidden()
                x_arrive(1, at_z(4))
                rs_a(2, 0)
                rs_a(2, 1)
            if (m, s) != (0, 0):
                ag_step(m, s)
            if s == 2 and m < 2:
                ag_first(m + 1)
            if s < 3:
                pair(m, s)
            else:
                block(m, at_z(4), last=True)
        exchange(m)

    over_cores(0)
    rs_b(2, 1)
    partial(0, core)
    rs(2, 2)
    over_x(0)
    rs(2, 3)
    make_grads()
    rs_a(0, 0)
    rs_a(0, 1)
    rs_last(2)
    over_cores(1)
    rs_b(0, 1)
    partial(1, core)
    rs(0, 2)
    over_x(1)
    over_yl(0)
    rs(0, 3)
    rs_a(1, 0)
    rs_a(1, 1)
    rs_last(0)
    to_owner(0)
    rs_b(1, 1)
    over_yl(1)
    rs(1, 2)
    out_last(0)
    to_owner(1)
    rs(1, 3)
    out_last(1)
    rs_last(1)
    for copy in sent:
        copy.wait_send()


def place(acts, grads, o_out, o_xg, o_gg, o_ug, o_dg, sems):
    copies = [pltpu.make_async_copy(acts.at[i], o, sems.at[i]) for i, o in enumerate((o_out, o_xg))]
    for m, o in enumerate((o_gg, o_ug, o_dg)):
        copies.append(pltpu.make_async_copy(grads.at[pl.ds(7 * m, 7)], o, sems.at[2 + m]))
    for copy in copies:
        copy.start()
    for copy in copies:
        copy.wait()


def on_device(x_in, out_grad, gate_tiles, up_tiles, down_tiles, gate_spot, up_spot, down_spot):
    vmem = pl.BlockSpec(memory_space=pltpu.VMEM)
    smem = pl.BlockSpec(memory_space=pltpu.SMEM)
    dma = pltpu.SemaphoreType.DMA
    anywhere = pl.BlockSpec(memory_space=pl.ANY)
    tile = jax.ShapeDtypeStruct((7, B, B), BF)
    act = jax.ShapeDtypeStruct((B, 256), BF)
    scratch = [
        pltpu.VMEM((NZ, 8, B), jnp.int32),
        pltpu.SMEM((NZ, 8, B), jnp.int32),
        pltpu.VMEM((NZ, 256, 256), BF),
        pltpu.VMEM((NZ, 256, 256), BF),
        pltpu.VMEM((NZ, 256, 256), BF),
        pltpu.VMEM((896, 256), BF),
        pltpu.VMEM((8, B, B), BF),
        pltpu.VMEM((3, NZ, 7, B, B), BF),
        pltpu.VMEM((NZ, 256, 896), BF),
        pltpu.VMEM((NZ, 256, 896), BF),
        pltpu.VMEM((NZ, 896, 256), BF),
        pltpu.VMEM((3, 256, 896), F32),
        pltpu.VMEM((3, 256, 896), BF),
        pltpu.VMEM((3, 256, 896), BF),
        pltpu.VMEM((256, 896), BF),
        pltpu.VMEM((256, 896), BF),
        pltpu.VMEM((256, 896), BF),
        pltpu.VMEM((3, 15, B, B), F32),
        pltpu.VMEM((3, 2, 4, 7, B, B), BF),
        pltpu.VMEM((3, 2, 4, 7, B, B), BF),
        pltpu.VMEM((2, 2, 4, 256, 256), BF),
        pltpu.VMEM((2, 4, 256, 256), BF),
        pltpu.VMEM((2, 4, 256, 256), BF),
        pltpu.VMEM((2, 3, 256, 256), BF),
        pltpu.VMEM((4, B, 256), F32),
        pltpu.VMEM((2, B, 256), BF),
        pltpu.VMEM((2, B, 256), BF),
        pltpu.VMEM((2, B, 256), BF),
        pltpu.VMEM((2, B, 256), BF),
        dma((7,)), dma((7,)), dma,
        dma((2, NZ)), dma((3,)),
        dma((2, NZ)), dma((2, NZ)),
        dma((3, 2, 4, 2)), dma((3, 2, 4, 2)),
        dma((3,)), dma((3,)),
        dma((3, 2, 4, 2)), dma((3, 2, 4, 2)),
        dma((2,)), dma((2,)),
        dma((2, 3)), dma((2, 3)),
        dma((2,)), dma((2,)),
        dma((2,)), dma((2,)),
    ]
    acts, grads = pl.pallas_call(
        kernel,
        out_shape=(jax.ShapeDtypeStruct((2, B, 256), BF), jax.ShapeDtypeStruct((21, B, B), BF)),
        in_specs=[anywhere] * 5 + [smem] * 3,
        out_specs=(vmem,) * 2,
        scratch_shapes=scratch,
        compiler_params=pltpu.CompilerParams(
            collective_id=0, has_side_effects=True, vmem_limit_bytes=60 * 2**20
        ),
        cost_estimate=pl.CostEstimate(flops=8_500_000_000, bytes_accessed=6_000_000, transcendentals=229_376),
        name="layer",
    )(x_in, out_grad, gate_tiles, up_tiles, down_tiles, gate_spot, up_spot, down_spot)
    return pl.pallas_call(
        place,
        out_shape=(act, act, tile, tile, tile),
        in_specs=[vmem] * 2,
        out_specs=(anywhere,) * 5,
        scratch_shapes=[dma((5,))],
        name="place",
    )(acts, grads)


def solution(mesh):
    blocks, spots = P(("dp", "feat"), None, None), P(("dp", "feat"))
    return jax.shard_map(
        on_device,
        mesh=mesh,
        in_specs=(P("dp", None),) * 2 + (blocks,) * 3 + (spots,) * 3,
        out_specs=(P("dp", "feat"),) * 2 + (blocks,) * 3,
        check_vma=False,
    )
```

```python
import jax
import jax.numpy as jnp
from jax import lax
from jax.experimental import pallas as pl
from jax.experimental.pallas import tpu as pltpu
from jax.sharding import PartitionSpec as P

BF, F32 = jnp.bfloat16, jnp.float32
B = 128
NZ = 8
CUT = ((0, 2), (2, 4), (4, 6), (6, 7))
NP, HALF = 4, 2
ORDER = (
    (0, 0), (0, 1), (1, 0), (0, 2), (1, 1), (0, 3), (1, 2), (1, 3),
    (2, 0), (2, 1), (2, 2), (2, 3),
)
MESH = pl.DeviceIdType.MESH


def dot(a, b):
    return lax.dot_general(a, b, (((1,), (0,)), ((), ())), preferred_element_type=F32)


def dot_nt(a, b):
    return lax.dot_general(a, b, (((1,), (1,)), ((), ())), preferred_element_type=F32)


def far(m, d):
    return range(HALF) if (d + (m == 1)) % 2 == 0 else range(HALF, NP)


def near(m, d):
    return [p for p in range(NP) if p not in far(m, d)]


def turns(m, pieces):
    lists = [list(pieces(m, d)) for d in range(2)]
    return [(d, lists[d][i]) for i in range(NP) for d in range(2) if i < len(lists[d])]


def every(m, d):
    return range(NP)


def kernel(
    x_ref, dy_ref, gt, ut, dt, gs, us, ds,
    o_act, o_grad,
    tabv, tabs, xk, dyk, xt, ht, stage, wb, wg, wu, wd, acc, ps, pr, hid, dg, du, grid,
    rss, rsr, ost, r1, s1, r2, s2f, s2b, r3, s3, r4,
    tab_ss, tab_rs, tab_ls, in_ls, w_ls, x_ss, x_rs, ag_ss, ag_rs, y_ss, y_rs, rs_ss, rs_rs,
    c_ss, c_rs, f_ss, f_rs, l_ss, l_rs, d_ss, d_rs,
):
    dp, ft = lax.axis_index("dp"), lax.axis_index("feat")
    yh, z = dp // 8, lax.rem(dp, 8)
    yl, xx, core = ft // 8, lax.rem(ft // 2, 4), lax.rem(ft, 2)

    def at_z(n):
        return lax.rem(z + (n % NZ), NZ)

    zdev = [(yh * 8 + at_z(1), ft), (yh * 8 + at_z(-1), ft)]
    zall = [(yh * 8 + at_z(n), ft) for n in range(1, NZ)]
    ydev = ((1 - yh) * 8 + z, ft)
    cdev = (dp, yl * 8 + xx * 2 + (1 - core))
    xdev = [(dp, yl * 8 + lax.rem(xx + n, 4) * 2 + core) for n in (1, 2, 3)]
    ldev = (dp, (1 - yl) * 8 + xx * 2 + core)
    ddev = ((1 - yh) * 8 + z, (1 - yl) * 8 + xx * 2 + core)

    barrier = pltpu.get_barrier_semaphore()
    peers = zall + [ydev, cdev] + xdev + [ldev, ddev]
    for dev in peers:
        pl.semaphore_signal(barrier, inc=1, device_id=dev, device_id_type=MESH)

    own = (gt, ut, dt)

    def in_copy(a, k):
        cols = pl.ds(pl.multiple_of((yh * 8 + k) * 256, 256), 256)
        return pltpu.make_async_copy((x_ref, dy_ref)[a].at[:, cols], (xk, dyk)[a].at[k, pl.ds(0, B)], in_ls.at[a, k])

    def w_copy(m):
        return pltpu.make_async_copy(own[m], wb.at[m, z], w_ls.at[m])

    for m in range(3):
        w_copy(m).start()
    for a in range(2):
        for k in range(NZ):
            in_copy(a, k).start()

    lane = lax.broadcasted_iota(jnp.int32, (8, B), 1)
    seg, q = lane >> 5, lane & 31
    tab = jnp.where(q < 14, 7, 14)
    for m, spots in enumerate((gs, us, ds)):
        for s in range(7):
            spot = spots[s]
            safe = jnp.maximum(spot, 0)
            if m < 2:
                place = (lax.div(safe, 112) - 2 * dp) * 7 + lax.rem(safe, 112) - 7 * ft
            else:
                place = (lax.div(safe, 32) - 7 * ft) * 2 + lax.rem(safe, 32) - 2 * dp
            place = jnp.where(spot >= 0, jnp.clip(place, 0, 13), 14)
            tab = jnp.where((seg == m) & (q < 14) & (q == place), s, tab)
            tab = jnp.where((seg == m) & (q == 16 + s), place, tab)
    tabv[z] = tab

    pl.semaphore_wait(barrier, len(peers))

    def rc(src, dst, ss, rs, dev):
        return pltpu.make_async_remote_copy(
            src_ref=src, dst_ref=dst, send_sem=ss, recv_sem=rs, device_id=dev, device_id_type=MESH
        )

    sent = []

    def go(copy):
        copy.start()
        sent.append(copy)

    w = (wg, wu, wd)

    def piece(p):
        return pl.ds(CUT[p][0], CUT[p][1] - CUT[p][0])

    def ag_send(m, d, s, p):
        o = at_z(-s if d == 0 else s)
        src = own[m].at[piece(p)] if s == 0 else wb.at[m, o, piece(p)]
        go(rc(src, wb.at[m, o, piece(p)], ag_ss.at[m, d, s, p], ag_rs.at[m, d, s, p], zdev[d]))

    def ag_arrive(m, d, s, p):
        o = at_z(-s - 1 if d == 0 else s + 1)
        here = wb.at[m, o, piece(p)]
        rc(here, here, ag_ss.at[m, d, s, p], ag_rs.at[m, d, s, p], zdev[d]).wait_recv()

    def ag_first(m):
        for d, p in turns(m, every):
            ag_send(m, d, 0, p)

    for i, dev in enumerate(zall):
        go(rc(tabv.at[z], tabv.at[z], tab_ss.at[i], tab_rs.at[i], dev))
    ag_first(0)
    order = (0, -1, 1, -2, 2, -3, 3, 4)
    for a, (src, dst) in enumerate(((x_ref, xk), (dy_ref, dyk))):
        for n in order:
            k = at_z(n)
            cols = pl.ds(pl.multiple_of(((1 - yh) * 8 + k) * 256, 256), 256)
            go(rc(src.at[:, cols], dst.at[k, pl.ds(B, B)], x_ss.at[a, k], x_rs.at[a, k], ydev))

    stage[7] = jnp.zeros((B, B), BF)
    for i in range(5):
        grid[i, 14] = jnp.zeros((B, B), F32)

    for i, n in enumerate(range(1, NZ)):
        here = tabv.at[at_z(-n)]
        rc(here, here, tab_ss.at[i], tab_rs.at[i], zall[i]).wait_recv()
    tabcopy = pltpu.make_async_copy(tabv, tabs, tab_ls)
    tabcopy.start()

    def x_arrive(a, k):
        dst = (xk, dyk)[a]
        here = dst.at[k, pl.ds(B, B)]
        in_copy(a, k).wait()
        rc(here, here, x_ss.at[a, k], x_rs.at[a, k], ydev).wait_recv()

    def block(m, o, first=False, last=False):
        if m == 0:
            x_arrive(0, o)
        if m == 2 and not last:
            x_arrive(1, o)
        if first:
            w_copy(m).wait()
        stage[0:7] = wb[m, o]
        cols = 7 if m < 2 else 2
        for p in range(14):
            r, c = divmod(p, cols)
            w[m][o, r * B : (r + 1) * B, c * B : (c + 1) * B] = stage[tabs[o, 0, m * 32 + p]]
        if m == 1:
            xt[o] = xk[o].T
        term = dot(xk[o], w[m][o]) if m < 2 else dot_nt(dyk[o], wd[o])
        if first:
            acc[m] = term
        else:
            acc[m] += term

    def pair(m, s):
        @pl.loop(0, 2)
        def _(d):
            block(m, lax.rem(z + NZ + (2 * d - 1) * (s + 1), NZ))

    def ag_step(m, s):
        for d, p in turns(m, far if s == 3 else every):
            ag_arrive(m, d, s, p)
            if s < 2 or (s == 2 and p in far(m, d)):
                ag_send(m, d, s + 1, p)

    def y_copy(m):
        return rc(ps.at[m], pr.at[m], y_ss.at[m], y_rs.at[m], ydev)

    def exchange(m):
        ps[m] = acc[m].astype(BF)
        go(y_copy(m))

    def halves(m, i):
        rows = pl.ds(pl.multiple_of(i * 16, 16), 16)
        rest = pl.ds(pl.multiple_of(i * 16 + B, 16), 16)
        return (
            (rows, acc[m, rows] + pr[m, rest].astype(F32)),
            (rest, acc[m, rest] + pr[m, rows].astype(F32)),
        )

    def make_hidden():
        y_copy(0).wait_recv()
        y_copy(1).wait_recv()

        @pl.loop(0, 8)
        def _(i):
            for (rows, g), (_, u) in zip(halves(0, i), halves(1, i)):
                sig = jax.nn.sigmoid(g)
                silu = g * sig
                hid[rows] = (silu * u).astype(BF)
                acc[0, rows] = u * sig * (1.0 + g * (1.0 - sig))
                acc[1, rows] = silu

        for i in range(7):
            ht[i * B : (i + 1) * B] = hid[:, i * B : (i + 1) * B].T

    def make_grads():
        y_copy(2).wait_recv()

        @pl.loop(0, 8)
        def _(i):
            for rows, dh in halves(2, i):
                dg[rows] = (dh * acc[0, rows]).astype(BF)
                du[rows] = (dh * acc[1, rows]).astype(BF)

    def grad_grid(m, k, i):
        if m == 2:
            term = dot(ht[...], dyk[k])
        else:
            term = dot(xt[k], (dg, du)[m][...])
        cols = 7 if m < 2 else 2
        for p in range(14):
            r, c = divmod(p, cols)
            grid[i, p] = term[r * B : (r + 1) * B, c * B : (c + 1) * B]

    def rs_copy(m, d, s, p):
        part = piece(p)
        return rc(
            rss.at[m, d, s, part], rsr.at[m, d, s, part],
            rs_ss.at[m, d, s, p], rs_rs.at[m, d, s, p], zdev[d],
        )

    def rs_send(m, d, s, p, k, i):
        add = s >= 2 or (s == 1 and p in far(m, d))
        if add:
            rs_copy(m, d, s - 1, p).wait_recv()
        for t in range(*CUT[p]):
            v = grid[i, tabs[k, 0, m * 32 + 16 + t]]
            if add:
                v = v + rsr[m, d, s - 1, t].astype(F32)
            rss[m, d, s, t] = v.astype(BF)
        go(rs_copy(m, d, s, p))

    def slot(m):
        return 2 if m == 1 else 0

    def rs_a(m, s):
        if s == 0:
            k = at_z(4)
            grad_grid(m, k, slot(m))
            for d, p in turns(m, far):
                rs_send(m, d, 0, p, k, slot(m))
            return
        for d in range(2):
            k = at_z(4 - s if d == 0 else 4 + s)
            grad_grid(m, k, slot(m) + d)
        for d, p in turns(m, near):
            k = at_z(4 - s if d == 0 else 4 + s)
            rs_send(m, d, s, p, k, slot(m) + d)

    def rs_b(m, s):
        for d, p in turns(m, far):
            k = at_z(4 - s if d == 0 else 4 + s)
            rs_send(m, d, s, p, k, slot(m) + d)

    def rs(m, s):
        rs_a(m, s)
        rs_b(m, s)

    def rs_last(m):
        grad_grid(m, z, 4)
        for d, p in turns(m, every):
            rs_copy(m, d, 3, p).wait_recv()
        for t in range(7):
            v = grid[4, tabs[z, 0, m * 32 + 16 + t]]
            v = v + rsr[m, 0, 3, t].astype(F32) + rsr[m, 1, 3, t].astype(F32)
            o_grad[m * 7 + t] = v.astype(BF)

    def partial(a, cc):
        @pl.loop(0, 4)
        def _(cx):
            k = 2 * cx + cc
            if a == 0:
                term = dot(hid[...], wd[k])
            else:
                term = dot_nt(dg[...], wg[k]) + dot_nt(du[...], wu[k])
            ost[a, cc, cx] = term.astype(BF)

    def c_copy(a):
        return rc(ost.at[a, 1 - core], r1.at[a], c_ss.at[a], c_rs.at[a], cdev)

    def f_copy(a, n):
        cx = lax.rem(xx + n, 4)
        return rc(s1.at[a, cx], r2.at[a, n - 1], f_ss.at[a, n - 1], f_rs.at[a, n - 1], xdev[n - 1])

    def l_copy(a):
        return rc(s2b.at[a], r3.at[a], l_ss.at[a], l_rs.at[a], ldev)

    def d_copy(a):
        return rc(s3.at[a], r4.at[a], d_ss.at[a], d_rs.at[a], ddev)

    def over_cores(a):
        partial(a, 1 - core)
        go(c_copy(a))

    def over_x(a):
        c_copy(a).wait_recv()
        for n in (2, 1, 3):
            cx = lax.rem(xx + n, 4)
            s1[a, cx] = (ost[a, core, cx].astype(F32) + r1[a, cx].astype(F32)).astype(BF)
            go(f_copy(a, n))

    give = lax.rem(yh + 1 - yl, 2)

    def over_yl(a):
        for n in (1, 2, 3):
            f_copy(a, n).wait_recv()
        for h in range(2):
            rows = slice(h * B, (h + 1) * B)
            v = ost[a, core, xx, rows].astype(F32) + r1[a, xx, rows].astype(F32)
            for n in range(3):
                v = v + r2[a, n, rows].astype(F32)
            s2f[h] = v
        s2b[a] = s2f[give].astype(BF)
        go(l_copy(a))
        s2f[2 + a] = s2f[1 - give]

    def to_owner(a):
        l_copy(a).wait_recv()
        s3[a] = (s2f[2 + a] + r3[a].astype(F32)).astype(BF)

        @pl.when(yh != yl)
        def _():
            d_copy(a).start()

    def out_last(a):
        @pl.when(yh != yl)
        def _():
            d_copy(a).wait()
            o_act[a] = r4[a]

        @pl.when(yh == yl)
        def _():
            o_act[a] = s3[a]

    for m, s in ORDER:
        if m == 2 and s == 3:
            make_hidden()
            x_arrive(1, at_z(4))
            rs_a(2, 0)
            rs_a(2, 1)
        ag_step(m, s)
        if (m, s) == (0, 0):
            tabcopy.wait()
        if (m, s) == (0, 0):
            ag_first(1)
        if (m, s) == (1, 2):
            ag_first(2)
        if s == 0:
            block(m, z, first=True)
        if s < 3:
            pair(m, s)
        else:
            block(m, at_z(4), last=True)
            exchange(m)

    over_cores(0)
    rs_b(2, 1)
    partial(0, core)
    rs(2, 2)
    over_x(0)
    rs(2, 3)
    make_grads()
    rs_a(0, 0)
    rs_a(1, 0)
    rs_a(0, 1)
    rs_last(2)
    rs_b(0, 1)
    rs_a(1, 1)
    rs_b(1, 1)
    over_cores(1)
    rs(0, 2)
    partial(1, core)
    rs(1, 2)
    over_x(1)
    over_yl(0)
    rs(0, 3)
    to_owner(0)
    rs(1, 3)
    over_yl(1)
    out_last(0)
    to_owner(1)
    rs_last(0)
    out_last(1)
    rs_last(1)
    for copy in sent:
        copy.wait_send()


def place(acts, grads, o_out, o_xg, o_gg, o_ug, o_dg, sems):
    copies = [pltpu.make_async_copy(acts.at[i], o, sems.at[i]) for i, o in enumerate((o_out, o_xg))]
    for m, o in enumerate((o_gg, o_ug, o_dg)):
        copies.append(pltpu.make_async_copy(grads.at[pl.ds(7 * m, 7)], o, sems.at[2 + m]))
    for copy in copies:
        copy.start()
    for copy in copies:
        copy.wait()


def on_device(x_in, out_grad, gate_tiles, up_tiles, down_tiles, gate_spot, up_spot, down_spot):
    vmem = pl.BlockSpec(memory_space=pltpu.VMEM)
    smem = pl.BlockSpec(memory_space=pltpu.SMEM)
    dma = pltpu.SemaphoreType.DMA
    anywhere = pl.BlockSpec(memory_space=pl.ANY)
    tile = jax.ShapeDtypeStruct((7, B, B), BF)
    act = jax.ShapeDtypeStruct((B, 256), BF)
    scratch = [
        pltpu.VMEM((NZ, 8, B), jnp.int32),
        pltpu.SMEM((NZ, 8, B), jnp.int32),
        pltpu.VMEM((NZ, 256, 256), BF),
        pltpu.VMEM((NZ, 256, 256), BF),
        pltpu.VMEM((NZ, 256, 256), BF),
        pltpu.VMEM((896, 256), BF),
        pltpu.VMEM((8, B, B), BF),
        pltpu.VMEM((3, NZ, 7, B, B), BF),
        pltpu.VMEM((NZ, 256, 896), BF),
        pltpu.VMEM((NZ, 256, 896), BF),
        pltpu.VMEM((NZ, 896, 256), BF),
        pltpu.VMEM((3, 256, 896), F32),
        pltpu.VMEM((3, 256, 896), BF),
        pltpu.VMEM((3, 256, 896), BF),
        pltpu.VMEM((256, 896), BF),
        pltpu.VMEM((256, 896), BF),
        pltpu.VMEM((256, 896), BF),
        pltpu.VMEM((5, 15, B, B), F32),
        pltpu.VMEM((3, 2, 4, 7, B, B), BF),
        pltpu.VMEM((3, 2, 4, 7, B, B), BF),
        pltpu.VMEM((2, 2, 4, 256, 256), BF),
        pltpu.VMEM((2, 4, 256, 256), BF),
        pltpu.VMEM((2, 4, 256, 256), BF),
        pltpu.VMEM((2, 3, 256, 256), BF),
        pltpu.VMEM((4, B, 256), F32),
        pltpu.VMEM((2, B, 256), BF),
        pltpu.VMEM((2, B, 256), BF),
        pltpu.VMEM((2, B, 256), BF),
        pltpu.VMEM((2, B, 256), BF),
        dma((7,)), dma((7,)), dma,
        dma((2, NZ)), dma((3,)),
        dma((2, NZ)), dma((2, NZ)),
        dma((3, 2, 4, NP)), dma((3, 2, 4, NP)),
        dma((3,)), dma((3,)),
        dma((3, 2, 4, NP)), dma((3, 2, 4, NP)),
        dma((2,)), dma((2,)),
        dma((2, 3)), dma((2, 3)),
        dma((2,)), dma((2,)),
        dma((2,)), dma((2,)),
    ]
    acts, grads = pl.pallas_call(
        kernel,
        out_shape=(jax.ShapeDtypeStruct((2, B, 256), BF), jax.ShapeDtypeStruct((21, B, B), BF)),
        in_specs=[anywhere] * 5 + [smem] * 3,
        out_specs=(vmem,) * 2,
        scratch_shapes=scratch,
        compiler_params=pltpu.CompilerParams(
            collective_id=0, has_side_effects=True, vmem_limit_bytes=60 * 2**20
        ),
        cost_estimate=pl.CostEstimate(flops=8_500_000_000, bytes_accessed=6_000_000, transcendentals=229_376),
        name="layer",
    )(x_in, out_grad, gate_tiles, up_tiles, down_tiles, gate_spot, up_spot, down_spot)
    return pl.pallas_call(
        place,
        out_shape=(act, act, tile, tile, tile),
        in_specs=[vmem] * 2,
        out_specs=(anywhere,) * 5,
        scratch_shapes=[dma((5,))],
        name="place",
    )(acts, grads)


def solution(mesh):
    blocks, spots = P(("dp", "feat"), None, None), P(("dp", "feat"))
    return jax.shard_map(
        on_device,
        mesh=mesh,
        in_specs=(P("dp", None),) * 2 + (blocks,) * 3 + (spots,) * 3,
        out_specs=(P("dp", "feat"),) * 2 + (blocks,) * 3,
        check_vma=False,
    )
```

```python
import jax
import jax.numpy as jnp
from jax import lax
from jax.experimental import pallas as pl
from jax.experimental.pallas import tpu as pltpu
from jax.sharding import PartitionSpec as P

BF, F32 = jnp.bfloat16, jnp.float32
B = 128
NZ = 8
CUT = ((0, 2), (2, 4), (4, 7))
NP, HALF = 3, 2
ORDER = (
    (0, 0), (0, 1), (1, 0), (0, 2), (1, 1), (0, 3), (1, 2), (1, 3),
    (2, 0), (2, 1), (2, 2), (2, 3),
)
MESH = pl.DeviceIdType.MESH


def dot(a, b):
    return lax.dot_general(a, b, (((1,), (0,)), ((), ())), preferred_element_type=F32)


def dot_nt(a, b):
    return lax.dot_general(a, b, (((1,), (1,)), ((), ())), preferred_element_type=F32)


def far(m, d):
    return range(HALF) if (d + (m == 1)) % 2 == 0 else range(HALF, NP)


def near(m, d):
    return [p for p in range(NP) if p not in far(m, d)]


def turns(m, pieces):
    lists = [list(pieces(m, d)) for d in range(2)]
    return [(d, lists[d][i]) for i in range(NP) for d in range(2) if i < len(lists[d])]


def every(m, d):
    return range(NP)


def kernel(
    x_ref, dy_ref, gt, ut, dt, gs, us, ds,
    o_act, o_grad,
    tabv, tabs, xk, dyk, xt, ht, stage, wb, wg, wu, wd, acc, ps, pr, hid, dg, du, grid,
    rss, rsr, ost, r1, s1, r2, s2f, s2b, r3, s3, r4,
    tab_ss, tab_rs, tab_ls, in_ls, w_ls, x_ss, x_rs, ag_ss, ag_rs, y_ss, y_rs, rs_ss, rs_rs,
    c_ss, c_rs, f_ss, f_rs, l_ss, l_rs, d_ss, d_rs,
):
    dp, ft = lax.axis_index("dp"), lax.axis_index("feat")
    yh, z = dp // 8, lax.rem(dp, 8)
    yl, xx, core = ft // 8, lax.rem(ft // 2, 4), lax.rem(ft, 2)

    def at_z(n):
        return lax.rem(z + (n % NZ), NZ)

    zdev = [(yh * 8 + at_z(1), ft), (yh * 8 + at_z(-1), ft)]
    ydev = ((1 - yh) * 8 + z, ft)
    cdev = (dp, yl * 8 + xx * 2 + (1 - core))
    xdev = [(dp, yl * 8 + lax.rem(xx + n, 4) * 2 + core) for n in (1, 2, 3)]
    ldev = (dp, (1 - yl) * 8 + xx * 2 + core)
    ddev = ((1 - yh) * 8 + z, (1 - yl) * 8 + xx * 2 + core)

    barrier = pltpu.get_barrier_semaphore()
    peers = zdev + [ydev, cdev] + xdev + [ldev, ddev]
    for dev in peers:
        pl.semaphore_signal(barrier, inc=1, device_id=dev, device_id_type=MESH)

    own = (gt, ut, dt)

    def in_copy(a, k):
        cols = pl.ds(pl.multiple_of((yh * 8 + k) * 256, 256), 256)
        return pltpu.make_async_copy((x_ref, dy_ref)[a].at[:, cols], (xk, dyk)[a].at[k, pl.ds(0, B)], in_ls.at[a, k])

    def w_copy(m):
        return pltpu.make_async_copy(own[m], wb.at[m, z], w_ls.at[m])

    for m in range(3):
        w_copy(m).start()
    for a in range(2):
        for k in range(NZ):
            in_copy(a, k).start()

    lane = lax.broadcasted_iota(jnp.int32, (8, B), 1)
    seg, q = lane >> 5, lane & 31
    tab = jnp.where(q < 14, 7, 14)
    for m, spots in enumerate((gs, us, ds)):
        for s in range(7):
            spot = spots[s]
            safe = jnp.maximum(spot, 0)
            if m < 2:
                place = (lax.div(safe, 112) - 2 * dp) * 7 + lax.rem(safe, 112) - 7 * ft
            else:
                place = (lax.div(safe, 32) - 7 * ft) * 2 + lax.rem(safe, 32) - 2 * dp
            place = jnp.where(spot >= 0, jnp.clip(place, 0, 13), 14)
            tab = jnp.where((seg == m) & (q < 14) & (q == place), s, tab)
            tab = jnp.where((seg == m) & (q == 16 + s), place, tab)
    tabv[z] = tab

    def tab_local(o):
        return pltpu.make_async_copy(tabv.at[o], tabs.at[o], tab_ls.at[o])

    tab_local(z).start()

    pl.semaphore_wait(barrier, len(peers))

    def rc(src, dst, ss, rs, dev):
        return pltpu.make_async_remote_copy(
            src_ref=src, dst_ref=dst, send_sem=ss, recv_sem=rs, device_id=dev, device_id_type=MESH
        )

    sent = []

    def go(copy):
        copy.start()
        sent.append(copy)

    w = (wg, wu, wd)

    def piece(p):
        return pl.ds(CUT[p][0], CUT[p][1] - CUT[p][0])

    def ag_send(m, d, s, p):
        o = at_z(-s if d == 0 else s)
        src = own[m].at[piece(p)] if s == 0 else wb.at[m, o, piece(p)]
        go(rc(src, wb.at[m, o, piece(p)], ag_ss.at[m, d, s, p], ag_rs.at[m, d, s, p], zdev[d]))

    def ag_arrive(m, d, s, p):
        o = at_z(-s - 1 if d == 0 else s + 1)
        here = wb.at[m, o, piece(p)]
        rc(here, here, ag_ss.at[m, d, s, p], ag_rs.at[m, d, s, p], zdev[d]).wait_recv()

    def ag_first(m):
        for d, p in turns(m, every):
            ag_send(m, d, 0, p)

    def tab_send(d, s):
        o = at_z(-s if d == 0 else s)
        go(rc(tabv.at[o], tabv.at[o], tab_ss.at[d, s], tab_rs.at[d, s], zdev[d]))

    def tab_step(s):
        for d in range(2 if s < 3 else 1):
            o = at_z(-s - 1 if d == 0 else s + 1)
            here = tabv.at[o]
            rc(here, here, tab_ss.at[d, s], tab_rs.at[d, s], zdev[d]).wait_recv()
            if s < 2 or (s == 2 and d == 0):
                tab_send(d, s + 1)
            tab_local(o).start()

    tab_send(0, 0)
    tab_send(1, 0)
    ag_first(0)
    order = (0, -1, 1, -2, 2, -3, 3, 4)
    for a, (src, dst) in enumerate(((x_ref, xk), (dy_ref, dyk))):
        for n in order:
            k = at_z(n)
            cols = pl.ds(pl.multiple_of(((1 - yh) * 8 + k) * 256, 256), 256)
            go(rc(src.at[:, cols], dst.at[k, pl.ds(B, B)], x_ss.at[a, k], x_rs.at[a, k], ydev))

    stage[7] = jnp.zeros((B, B), BF)
    for i in range(5):
        grid[i, 14] = jnp.zeros((B, B), F32)

    def x_arrive(a, k):
        dst = (xk, dyk)[a]
        here = dst.at[k, pl.ds(B, B)]
        in_copy(a, k).wait()
        rc(here, here, x_ss.at[a, k], x_rs.at[a, k], ydev).wait_recv()

    def block(m, o, first=False, last=False):
        if m == 0:
            tab_local(o).wait()
            x_arrive(0, o)
        if m == 2 and not last:
            x_arrive(1, o)
        if first:
            w_copy(m).wait()
        stage[0:7] = wb[m, o]
        cols = 7 if m < 2 else 2
        for p in range(14):
            r, c = divmod(p, cols)
            w[m][o, r * B : (r + 1) * B, c * B : (c + 1) * B] = stage[tabs[o, 0, m * 32 + p]]
        if m == 1:
            xt[o] = xk[o].T
        term = dot(xk[o], w[m][o]) if m < 2 else dot_nt(dyk[o], wd[o])
        if first:
            acc[m] = term
        else:
            acc[m] += term

    def pair(m, s):
        @pl.loop(0, 2)
        def _(d):
            block(m, lax.rem(z + NZ + (2 * d - 1) * (s + 1), NZ))

    def ag_step(m, s):
        for d, p in turns(m, far if s == 3 else every):
            ag_arrive(m, d, s, p)
            if s < 2 or (s == 2 and p in far(m, d)):
                ag_send(m, d, s + 1, p)

    def y_copy(m):
        return rc(ps.at[m], pr.at[m], y_ss.at[m], y_rs.at[m], ydev)

    def exchange(m):
        ps[m] = acc[m].astype(BF)
        go(y_copy(m))

    def halves(m, i):
        rows = pl.ds(pl.multiple_of(i * 16, 16), 16)
        rest = pl.ds(pl.multiple_of(i * 16 + B, 16), 16)
        return (
            (rows, acc[m, rows] + pr[m, rest].astype(F32)),
            (rest, acc[m, rest] + pr[m, rows].astype(F32)),
        )

    def make_hidden():
        y_copy(0).wait_recv()
        y_copy(1).wait_recv()

        @pl.loop(0, 8)
        def _(i):
            for (rows, g), (_, u) in zip(halves(0, i), halves(1, i)):
                sig = jax.nn.sigmoid(g)
                silu = g * sig
                hid[rows] = (silu * u).astype(BF)
                acc[0, rows] = u * sig * (1.0 + g * (1.0 - sig))
                acc[1, rows] = silu

        for i in range(7):
            ht[i * B : (i + 1) * B] = hid[:, i * B : (i + 1) * B].T

    def make_grads():
        y_copy(2).wait_recv()

        @pl.loop(0, 8)
        def _(i):
            for rows, dh in halves(2, i):
                dg[rows] = (dh * acc[0, rows]).astype(BF)
                du[rows] = (dh * acc[1, rows]).astype(BF)

    def grad_grid(m, k, i):
        if m == 2:
            term = dot(ht[...], dyk[k])
        else:
            term = dot(xt[k], (dg, du)[m][...])
        cols = 7 if m < 2 else 2
        for p in range(14):
            r, c = divmod(p, cols)
            grid[i, p] = term[r * B : (r + 1) * B, c * B : (c + 1) * B]

    def rs_copy(m, d, s, p):
        part = piece(p)
        return rc(
            rss.at[m, d, s, part], rsr.at[m, d, s, part],
            rs_ss.at[m, d, s, p], rs_rs.at[m, d, s, p], zdev[d],
        )

    def rs_send(m, d, s, p, k, i):
        add = s >= 2 or (s == 1 and p in far(m, d))
        if add:
            rs_copy(m, d, s - 1, p).wait_recv()
        for t in range(*CUT[p]):
            v = grid[i, tabs[k, 0, m * 32 + 16 + t]]
            if add:
                v = v + rsr[m, d, s - 1, t].astype(F32)
            rss[m, d, s, t] = v.astype(BF)
        go(rs_copy(m, d, s, p))

    def slot(m):
        return 2 if m == 1 else 0

    def rs_a(m, s):
        if s == 0:
            k = at_z(4)
            grad_grid(m, k, slot(m))
            for d, p in turns(m, far):
                rs_send(m, d, 0, p, k, slot(m))
            return
        for d in range(2):
            k = at_z(4 - s if d == 0 else 4 + s)
            grad_grid(m, k, slot(m) + d)
        for d, p in turns(m, near):
            k = at_z(4 - s if d == 0 else 4 + s)
            rs_send(m, d, s, p, k, slot(m) + d)

    def rs_b(m, s):
        for d, p in turns(m, far):
            k = at_z(4 - s if d == 0 else 4 + s)
            rs_send(m, d, s, p, k, slot(m) + d)

    def rs(m, s):
        rs_a(m, s)
        rs_b(m, s)

    def rs_last(m, i):
        for p in range(NP):
            for d in range(2):
                rs_copy(m, d, 3, p).wait_recv()
            for t in range(*CUT[p]):
                v = grid[i, tabs[z, 0, m * 32 + 16 + t]]
                v = v + rsr[m, 0, 3, t].astype(F32) + rsr[m, 1, 3, t].astype(F32)
                o_grad[m * 7 + t] = v.astype(BF)

    def partial(a, cc):
        @pl.loop(0, 4)
        def _(cx):
            k = 2 * cx + cc
            if a == 0:
                term = dot(hid[...], wd[k])
            else:
                term = dot_nt(dg[...], wg[k]) + dot_nt(du[...], wu[k])
            ost[a, cc, cx] = term.astype(BF)

    def c_copy(a):
        return rc(ost.at[a, 1 - core], r1.at[a], c_ss.at[a], c_rs.at[a], cdev)

    def f_copy(a, n):
        cx = lax.rem(xx + n, 4)
        return rc(s1.at[a, cx], r2.at[a, n - 1], f_ss.at[a, n - 1], f_rs.at[a, n - 1], xdev[n - 1])

    def l_copy(a):
        return rc(s2b.at[a], r3.at[a], l_ss.at[a], l_rs.at[a], ldev)

    def d_copy(a):
        return rc(s3.at[a], r4.at[a], d_ss.at[a], d_rs.at[a], ddev)

    def over_cores(a):
        partial(a, 1 - core)
        go(c_copy(a))

    def over_x(a):
        c_copy(a).wait_recv()
        for n in (2, 1, 3):
            cx = lax.rem(xx + n, 4)
            s1[a, cx] = (ost[a, core, cx].astype(F32) + r1[a, cx].astype(F32)).astype(BF)
            go(f_copy(a, n))

    give = lax.rem(yh + 1 - yl, 2)

    def over_yl(a):
        for n in (1, 2, 3):
            f_copy(a, n).wait_recv()
        for h in range(2):
            rows = slice(h * B, (h + 1) * B)
            v = ost[a, core, xx, rows].astype(F32) + r1[a, xx, rows].astype(F32)
            for n in range(3):
                v = v + r2[a, n, rows].astype(F32)
            s2f[h] = v
        s2b[a] = s2f[give].astype(BF)
        go(l_copy(a))
        s2f[2 + a] = s2f[1 - give]

    def to_owner(a):
        l_copy(a).wait_recv()
        s3[a] = (s2f[2 + a] + r3[a].astype(F32)).astype(BF)

        @pl.when(yh != yl)
        def _():
            d_copy(a).start()

    def out_last(a):
        @pl.when(yh != yl)
        def _():
            d_copy(a).wait()
            o_act[a] = r4[a]

        @pl.when(yh == yl)
        def _():
            o_act[a] = s3[a]

    for m, s in ORDER:
        if m == 2 and s == 3:
            make_hidden()
            x_arrive(1, at_z(4))
            rs_a(2, 0)
            rs_a(2, 1)
        if m == 0:
            tab_step(s)
        ag_step(m, s)
        if (m, s) == (0, 0):
            ag_first(1)
        if (m, s) == (1, 2):
            ag_first(2)
        if s == 0:
            block(m, z, first=True)
        if s < 3:
            pair(m, s)
        else:
            block(m, at_z(4), last=True)
            exchange(m)

    over_cores(0)
    rs_b(2, 1)
    partial(0, core)
    rs(2, 2)
    over_x(0)
    rs(2, 3)
    make_grads()
    rs_a(0, 0)
    rs_a(1, 0)
    rs_a(0, 1)
    rs_a(1, 1)
    rs_b(0, 1)
    rs_b(1, 1)
    grad_grid(2, z, 4)
    rs_last(2, 4)
    over_cores(1)
    rs(0, 2)
    partial(1, core)
    rs(1, 2)
    over_x(1)
    over_yl(0)
    rs(0, 3)
    to_owner(0)
    rs(1, 3)
    over_yl(1)
    out_last(0)
    to_owner(1)
    out_last(1)
    grad_grid(0, z, 4)
    grad_grid(1, z, 0)
    rs_last(0, 4)
    rs_last(1, 0)
    for copy in sent:
        copy.wait_send()


def place(acts, grads, o_out, o_xg, o_gg, o_ug, o_dg, sems):
    copies = [pltpu.make_async_copy(acts.at[i], o, sems.at[i]) for i, o in enumerate((o_out, o_xg))]
    for m, o in enumerate((o_gg, o_ug, o_dg)):
        copies.append(pltpu.make_async_copy(grads.at[pl.ds(7 * m, 7)], o, sems.at[2 + m]))
    for copy in copies:
        copy.start()
    for copy in copies:
        copy.wait()


def on_device(x_in, out_grad, gate_tiles, up_tiles, down_tiles, gate_spot, up_spot, down_spot):
    vmem = pl.BlockSpec(memory_space=pltpu.VMEM)
    smem = pl.BlockSpec(memory_space=pltpu.SMEM)
    dma = pltpu.SemaphoreType.DMA
    anywhere = pl.BlockSpec(memory_space=pl.ANY)
    tile = jax.ShapeDtypeStruct((7, B, B), BF)
    act = jax.ShapeDtypeStruct((B, 256), BF)
    scratch = [
        pltpu.VMEM((NZ, 8, B), jnp.int32),
        pltpu.SMEM((NZ, 8, B), jnp.int32),
        pltpu.VMEM((NZ, 256, 256), BF),
        pltpu.VMEM((NZ, 256, 256), BF),
        pltpu.VMEM((NZ, 256, 256), BF),
        pltpu.VMEM((896, 256), BF),
        pltpu.VMEM((8, B, B), BF),
        pltpu.VMEM((3, NZ, 7, B, B), BF),
        pltpu.VMEM((NZ, 256, 896), BF),
        pltpu.VMEM((NZ, 256, 896), BF),
        pltpu.VMEM((NZ, 896, 256), BF),
        pltpu.VMEM((3, 256, 896), F32),
        pltpu.VMEM((3, 256, 896), BF),
        pltpu.VMEM((3, 256, 896), BF),
        pltpu.VMEM((256, 896), BF),
        pltpu.VMEM((256, 896), BF),
        pltpu.VMEM((256, 896), BF),
        pltpu.VMEM((5, 15, B, B), F32),
        pltpu.VMEM((3, 2, 4, 7, B, B), BF),
        pltpu.VMEM((3, 2, 4, 7, B, B), BF),
        pltpu.VMEM((2, 2, 4, 256, 256), BF),
        pltpu.VMEM((2, 4, 256, 256), BF),
        pltpu.VMEM((2, 4, 256, 256), BF),
        pltpu.VMEM((2, 3, 256, 256), BF),
        pltpu.VMEM((4, B, 256), F32),
        pltpu.VMEM((2, B, 256), BF),
        pltpu.VMEM((2, B, 256), BF),
        pltpu.VMEM((2, B, 256), BF),
        pltpu.VMEM((2, B, 256), BF),
        dma((2, 4)), dma((2, 4)), dma((NZ,)),
        dma((2, NZ)), dma((3,)),
        dma((2, NZ)), dma((2, NZ)),
        dma((3, 2, 4, NP)), dma((3, 2, 4, NP)),
        dma((3,)), dma((3,)),
        dma((3, 2, 4, NP)), dma((3, 2, 4, NP)),
        dma((2,)), dma((2,)),
        dma((2, 3)), dma((2, 3)),
        dma((2,)), dma((2,)),
        dma((2,)), dma((2,)),
    ]
    acts, grads = pl.pallas_call(
        kernel,
        out_shape=(jax.ShapeDtypeStruct((2, B, 256), BF), jax.ShapeDtypeStruct((21, B, B), BF)),
        in_specs=[anywhere] * 5 + [smem] * 3,
        out_specs=(vmem,) * 2,
        scratch_shapes=scratch,
        compiler_params=pltpu.CompilerParams(
            collective_id=0, has_side_effects=True, vmem_limit_bytes=60 * 2**20
        ),
        cost_estimate=pl.CostEstimate(flops=8_500_000_000, bytes_accessed=6_000_000, transcendentals=229_376),
        name="layer",
    )(x_in, out_grad, gate_tiles, up_tiles, down_tiles, gate_spot, up_spot, down_spot)
    return pl.pallas_call(
        place,
        out_shape=(act, act, tile, tile, tile),
        in_specs=[vmem] * 2,
        out_specs=(anywhere,) * 5,
        scratch_shapes=[dma((5,))],
        name="place",
    )(acts, grads)


def solution(mesh):
    blocks, spots = P(("dp", "feat"), None, None), P(("dp", "feat"))
    return jax.shard_map(
        on_device,
        mesh=mesh,
        in_specs=(P("dp", None),) * 2 + (blocks,) * 3 + (spots,) * 3,
        out_specs=(P("dp", "feat"),) * 2 + (blocks,) * 3,
        check_vma=False,
    )
```

```python
import jax
import jax.numpy as jnp
from jax import lax
from jax.experimental import pallas as pl
from jax.experimental.pallas import tpu as pltpu
from jax.sharding import PartitionSpec as P

BF, F32 = jnp.bfloat16, jnp.float32
B = 128
NZ = 8
CUT = ((0, 2), (2, 4), (4, 7))
NP, HALF = 3, 2
ORDER = (
    (0, 0), (0, 1), (1, 0), (0, 2), (1, 1), (0, 3), (1, 2), (1, 3),
    (2, 0), (2, 1), (2, 2), (2, 3),
)
MESH = pl.DeviceIdType.MESH


def dot(a, b):
    return lax.dot_general(a, b, (((1,), (0,)), ((), ())), preferred_element_type=F32)


def dot_nt(a, b):
    return lax.dot_general(a, b, (((1,), (1,)), ((), ())), preferred_element_type=F32)


def far(m, d):
    return range(HALF) if (d + (m == 1)) % 2 == 0 else range(HALF, NP)


def near(m, d):
    return [p for p in range(NP) if p not in far(m, d)]


def turns(m, pieces):
    lists = [list(pieces(m, d)) for d in range(2)]
    return [(d, lists[d][i]) for i in range(NP) for d in range(2) if i < len(lists[d])]


def every(m, d):
    return range(NP)


def kernel(
    x_ref, dy_ref, gt, ut, dt, gs, us, ds,
    o_act, o_grad,
    tabv, tabs, xk, dyk, xt, ht, stage, wb, wg, wu, wd, acc, ps, pr, hid, dg, du, grid,
    rss, rsr, ost, r1, s1, r2, s2f, s2b, r3, s3, r4,
    tab_ss, tab_rs, tab_ls, in_ls, w_ls, x_ss, x_rs, ag_ss, ag_rs, y_ss, y_rs, rs_ss, rs_rs,
    c_ss, c_rs, f_ss, f_rs, l_ss, l_rs, d_ss, d_rs,
):
    dp, ft = lax.axis_index("dp"), lax.axis_index("feat")
    yh, z = dp // 8, lax.rem(dp, 8)
    yl, xx, core = ft // 8, lax.rem(ft // 2, 4), lax.rem(ft, 2)

    def at_z(n):
        return lax.rem(z + (n % NZ), NZ)

    zdev = [(yh * 8 + at_z(1), ft), (yh * 8 + at_z(-1), ft)]
    ydev = ((1 - yh) * 8 + z, ft)
    cdev = (dp, yl * 8 + xx * 2 + (1 - core))
    xdev = [(dp, yl * 8 + lax.rem(xx + n, 4) * 2 + core) for n in (1, 2, 3)]
    ldev = (dp, (1 - yl) * 8 + xx * 2 + core)
    ddev = ((1 - yh) * 8 + z, (1 - yl) * 8 + xx * 2 + core)

    barrier = pltpu.get_barrier_semaphore()
    peers = zdev + [ydev, cdev] + xdev + [ldev, ddev]
    for dev in peers:
        pl.semaphore_signal(barrier, inc=1, device_id=dev, device_id_type=MESH)

    own = (gt, ut, dt)

    def in_copy(a, k):
        cols = pl.ds(pl.multiple_of((yh * 8 + k) * 256, 256), 256)
        return pltpu.make_async_copy((x_ref, dy_ref)[a].at[:, cols], (xk, dyk)[a].at[k, pl.ds(0, B)], in_ls.at[a, k])

    def w_copy(m):
        return pltpu.make_async_copy(own[m], wb.at[m, z], w_ls.at[m])

    for m in range(3):
        w_copy(m).start()
    for a in range(2):
        for k in range(NZ):
            in_copy(a, k).start()

    lane = lax.broadcasted_iota(jnp.int32, (8, B), 1)
    seg, q = lane >> 5, lane & 31
    tab = jnp.where(q < 14, 7, 14)
    for m, spots in enumerate((gs, us, ds)):
        for s in range(7):
            spot = spots[s]
            safe = jnp.maximum(spot, 0)
            if m < 2:
                place = (lax.div(safe, 112) - 2 * dp) * 7 + lax.rem(safe, 112) - 7 * ft
            else:
                place = (lax.div(safe, 32) - 7 * ft) * 2 + lax.rem(safe, 32) - 2 * dp
            place = jnp.where(spot >= 0, jnp.clip(place, 0, 13), 14)
            tab = jnp.where((seg == m) & (q < 14) & (q == place), s, tab)
            tab = jnp.where((seg == m) & (q == 16 + s), place, tab)
    tabv[z] = tab

    def tab_local(o):
        return pltpu.make_async_copy(tabv.at[o], tabs.at[o], tab_ls.at[o])

    tab_local(z).start()

    pl.semaphore_wait(barrier, len(peers))

    def rc(src, dst, ss, rs, dev):
        return pltpu.make_async_remote_copy(
            src_ref=src, dst_ref=dst, send_sem=ss, recv_sem=rs, device_id=dev, device_id_type=MESH
        )

    sent = []

    def go(copy):
        copy.start()
        sent.append(copy)

    w = (wg, wu, wd)

    def piece(p):
        return pl.ds(CUT[p][0], CUT[p][1] - CUT[p][0])

    def ag_send(m, d, s, p):
        o = at_z(-s if d == 0 else s)
        src = own[m].at[piece(p)] if s == 0 else wb.at[m, o, piece(p)]
        go(rc(src, wb.at[m, o, piece(p)], ag_ss.at[m, d, s, p], ag_rs.at[m, d, s, p], zdev[d]))

    def ag_arrive(m, d, s, p):
        o = at_z(-s - 1 if d == 0 else s + 1)
        here = wb.at[m, o, piece(p)]
        rc(here, here, ag_ss.at[m, d, s, p], ag_rs.at[m, d, s, p], zdev[d]).wait_recv()

    def ag_first(m):
        for d, p in turns(m, every):
            ag_send(m, d, 0, p)

    def tab_send(d, s):
        o = at_z(-s if d == 0 else s)
        go(rc(tabv.at[o], tabv.at[o], tab_ss.at[d, s], tab_rs.at[d, s], zdev[d]))

    def tab_step(s):
        for d in range(2 if s < 3 else 1):
            o = at_z(-s - 1 if d == 0 else s + 1)
            here = tabv.at[o]
            rc(here, here, tab_ss.at[d, s], tab_rs.at[d, s], zdev[d]).wait_recv()
            if s < 2 or (s == 2 and d == 0):
                tab_send(d, s + 1)
            tab_local(o).start()

    tab_send(0, 0)
    tab_send(1, 0)
    ag_first(0)
    order = (0, -1, 1, -2, 2, -3, 3, 4)
    for a, (src, dst) in enumerate(((x_ref, xk), (dy_ref, dyk))):
        for n in order:
            k = at_z(n)
            cols = pl.ds(pl.multiple_of(((1 - yh) * 8 + k) * 256, 256), 256)
            go(rc(src.at[:, cols], dst.at[k, pl.ds(B, B)], x_ss.at[a, k], x_rs.at[a, k], ydev))

    stage[7] = jnp.zeros((B, B), BF)
    for i in range(5):
        grid[i, 14] = jnp.zeros((B, B), F32)

    def x_arrive(a, k):
        dst = (xk, dyk)[a]
        here = dst.at[k, pl.ds(B, B)]
        in_copy(a, k).wait()
        rc(here, here, x_ss.at[a, k], x_rs.at[a, k], ydev).wait_recv()

    def block(m, o, first=False, last=False):
        if m == 0:
            tab_local(o).wait()
            x_arrive(0, o)
        if m == 2 and not last:
            x_arrive(1, o)
        if first:
            w_copy(m).wait()
        stage[0:7] = wb[m, o]
        cols = 7 if m < 2 else 2
        for p in range(14):
            r, c = divmod(p, cols)
            w[m][o, r * B : (r + 1) * B, c * B : (c + 1) * B] = stage[tabs[o, 0, m * 32 + p]]
        if m == 1:
            xt[o] = xk[o].T
        term = dot(xk[o], w[m][o]) if m < 2 else dot_nt(dyk[o], wd[o])
        if first:
            acc[m] = term
        else:
            acc[m] += term

    def pair(m, s):
        @pl.loop(0, 2)
        def _(d):
            block(m, lax.rem(z + NZ + (2 * d - 1) * (s + 1), NZ))

    def ag_step(m, s):
        for d, p in turns(m, far if s == 3 else every):
            ag_arrive(m, d, s, p)
            if s < 2 or (s == 2 and p in far(m, d)):
                ag_send(m, d, s + 1, p)

    def y_copy(m):
        return rc(ps.at[m], pr.at[m], y_ss.at[m], y_rs.at[m], ydev)

    def exchange(m):
        ps[m] = acc[m].astype(BF)
        go(y_copy(m))

    def halves(m, i):
        rows = pl.ds(pl.multiple_of(i * 16, 16), 16)
        rest = pl.ds(pl.multiple_of(i * 16 + B, 16), 16)
        return (
            (rows, acc[m, rows] + pr[m, rest].astype(F32)),
            (rest, acc[m, rest] + pr[m, rows].astype(F32)),
        )

    def make_hidden():
        y_copy(0).wait_recv()
        y_copy(1).wait_recv()

        @pl.loop(0, 8)
        def _(i):
            for (rows, g), (_, u) in zip(halves(0, i), halves(1, i)):
                sig = jax.nn.sigmoid(g)
                silu = g * sig
                hid[rows] = (silu * u).astype(BF)
                acc[0, rows] = u * sig * (1.0 + g * (1.0 - sig))
                acc[1, rows] = silu

        for i in range(7):
            ht[i * B : (i + 1) * B] = hid[:, i * B : (i + 1) * B].T

    def make_grad(m):
        @pl.loop(0, 8)
        def _(i):
            for rows, dh in halves(2, i):
                (dg, du)[m][rows] = (dh * acc[m, rows]).astype(BF)

    def grad_grid(m, k, i):
        if m == 2:
            term = dot(ht[...], dyk[k])
        else:
            term = dot(xt[k], (dg, du)[m][...])
        cols = 7 if m < 2 else 2
        for p in range(14):
            r, c = divmod(p, cols)
            grid[i, p] = term[r * B : (r + 1) * B, c * B : (c + 1) * B]

    def rs_copy(m, d, s, p):
        part = piece(p)
        return rc(
            rss.at[m, d, s, part], rsr.at[m, d, s, part],
            rs_ss.at[m, d, s, p], rs_rs.at[m, d, s, p], zdev[d],
        )

    def rs_send(m, d, s, p, k, i):
        add = s >= 2 or (s == 1 and p in far(m, d))
        if add:
            rs_copy(m, d, s - 1, p).wait_recv()
        for t in range(*CUT[p]):
            v = grid[i, tabs[k, 0, m * 32 + 16 + t]]
            if add:
                v = v + rsr[m, d, s - 1, t].astype(F32)
            rss[m, d, s, t] = v.astype(BF)
        go(rs_copy(m, d, s, p))

    def slot(m):
        return 2 if m == 1 else 0

    def rs_a(m, s):
        if s == 0:
            k = at_z(4)
            grad_grid(m, k, slot(m))
            for d, p in turns(m, far):
                rs_send(m, d, 0, p, k, slot(m))
            return
        for d in range(2):
            k = at_z(4 - s if d == 0 else 4 + s)
            grad_grid(m, k, slot(m) + d)
        for d, p in turns(m, near):
            k = at_z(4 - s if d == 0 else 4 + s)
            rs_send(m, d, s, p, k, slot(m) + d)

    def rs_b(m, s):
        for d, p in turns(m, far):
            k = at_z(4 - s if d == 0 else 4 + s)
            rs_send(m, d, s, p, k, slot(m) + d)

    def rs(m, s):
        rs_a(m, s)
        rs_b(m, s)

    def rs_last(m, i):
        for p in range(NP):
            for d in range(2):
                rs_copy(m, d, 3, p).wait_recv()
            for t in range(*CUT[p]):
                v = grid[i, tabs[z, 0, m * 32 + 16 + t]]
                v = v + rsr[m, 0, 3, t].astype(F32) + rsr[m, 1, 3, t].astype(F32)
                o_grad[m * 7 + t] = v.astype(BF)

    def partial(a, cc):
        @pl.loop(0, 4)
        def _(cx):
            k = 2 * cx + cc
            if a == 0:
                term = dot(hid[...], wd[k])
            else:
                term = dot_nt(dg[...], wg[k]) + dot_nt(du[...], wu[k])
            ost[a, cc, cx] = term.astype(BF)

    def c_copy(a):
        return rc(ost.at[a, 1 - core], r1.at[a], c_ss.at[a], c_rs.at[a], cdev)

    def f_copy(a, n):
        cx = lax.rem(xx + n, 4)
        return rc(s1.at[a, cx], r2.at[a, n - 1], f_ss.at[a, n - 1], f_rs.at[a, n - 1], xdev[n - 1])

    def l_copy(a):
        return rc(s2b.at[a], r3.at[a], l_ss.at[a], l_rs.at[a], ldev)

    def d_copy(a):
        return rc(s3.at[a], r4.at[a], d_ss.at[a], d_rs.at[a], ddev)

    def over_cores(a):
        partial(a, 1 - core)
        go(c_copy(a))

    def over_x(a):
        c_copy(a).wait_recv()
        for n in (2, 1, 3):
            cx = lax.rem(xx + n, 4)
            s1[a, cx] = (ost[a, core, cx].astype(F32) + r1[a, cx].astype(F32)).astype(BF)
            go(f_copy(a, n))

    give = lax.rem(yh + 1 - yl, 2)

    def over_yl(a):
        for n in (1, 2, 3):
            f_copy(a, n).wait_recv()
        for h in range(2):
            rows = slice(h * B, (h + 1) * B)
            v = ost[a, core, xx, rows].astype(F32) + r1[a, xx, rows].astype(F32)
            for n in range(3):
                v = v + r2[a, n, rows].astype(F32)
            s2f[h] = v
        s2b[a] = s2f[give].astype(BF)
        go(l_copy(a))
        s2f[2 + a] = s2f[1 - give]

    def to_owner(a):
        l_copy(a).wait_recv()
        s3[a] = (s2f[2 + a] + r3[a].astype(F32)).astype(BF)

        @pl.when(yh != yl)
        def _():
            d_copy(a).start()

    def out_last(a):
        @pl.when(yh != yl)
        def _():
            d_copy(a).wait()
            o_act[a] = r4[a]

        @pl.when(yh == yl)
        def _():
            o_act[a] = s3[a]

    for m, s in ORDER:
        if m == 2 and s == 3:
            make_hidden()
            x_arrive(1, at_z(4))
            rs_a(2, 0)
            rs_a(2, 1)
        if m == 0:
            tab_step(s)
        ag_step(m, s)
        if (m, s) == (0, 0):
            ag_first(1)
        if (m, s) == (1, 2):
            ag_first(2)
        if s == 0:
            block(m, z, first=True)
        if s < 3:
            pair(m, s)
        else:
            block(m, at_z(4), last=True)
            exchange(m)

    over_cores(0)
    rs_b(2, 1)
    partial(0, core)
    rs(2, 2)
    over_x(0)
    rs(2, 3)
    y_copy(2).wait_recv()
    make_grad(0)
    rs_a(0, 0)
    make_grad(1)
    rs_a(1, 0)
    rs_a(0, 1)
    rs_a(1, 1)
    rs_b(0, 1)
    rs_b(1, 1)
    grad_grid(2, z, 4)
    rs_last(2, 4)
    over_cores(1)
    rs(0, 2)
    partial(1, core)
    rs(1, 2)
    over_x(1)
    over_yl(0)
    rs(0, 3)
    to_owner(0)
    rs(1, 3)
    over_yl(1)
    out_last(0)
    to_owner(1)
    out_last(1)
    grad_grid(0, z, 4)
    grad_grid(1, z, 0)
    rs_last(0, 4)
    rs_last(1, 0)
    for copy in sent:
        copy.wait_send()


def place(acts, grads, o_out, o_xg, o_gg, o_ug, o_dg, sems):
    copies = [pltpu.make_async_copy(acts.at[i], o, sems.at[i]) for i, o in enumerate((o_out, o_xg))]
    for m, o in enumerate((o_gg, o_ug, o_dg)):
        copies.append(pltpu.make_async_copy(grads.at[pl.ds(7 * m, 7)], o, sems.at[2 + m]))
    for copy in copies:
        copy.start()
    for copy in copies:
        copy.wait()


def on_device(x_in, out_grad, gate_tiles, up_tiles, down_tiles, gate_spot, up_spot, down_spot):
    vmem = pl.BlockSpec(memory_space=pltpu.VMEM)
    smem = pl.BlockSpec(memory_space=pltpu.SMEM)
    dma = pltpu.SemaphoreType.DMA
    anywhere = pl.BlockSpec(memory_space=pl.ANY)
    tile = jax.ShapeDtypeStruct((7, B, B), BF)
    act = jax.ShapeDtypeStruct((B, 256), BF)
    scratch = [
        pltpu.VMEM((NZ, 8, B), jnp.int32),
        pltpu.SMEM((NZ, 8, B), jnp.int32),
        pltpu.VMEM((NZ, 256, 256), BF),
        pltpu.VMEM((NZ, 256, 256), BF),
        pltpu.VMEM((NZ, 256, 256), BF),
        pltpu.VMEM((896, 256), BF),
        pltpu.VMEM((8, B, B), BF),
        pltpu.VMEM((3, NZ, 7, B, B), BF),
        pltpu.VMEM((NZ, 256, 896), BF),
        pltpu.VMEM((NZ, 256, 896), BF),
        pltpu.VMEM((NZ, 896, 256), BF),
        pltpu.VMEM((3, 256, 896), F32),
        pltpu.VMEM((3, 256, 896), BF),
        pltpu.VMEM((3, 256, 896), BF),
        pltpu.VMEM((256, 896), BF),
        pltpu.VMEM((256, 896), BF),
        pltpu.VMEM((256, 896), BF),
        pltpu.VMEM((5, 15, B, B), F32),
        pltpu.VMEM((3, 2, 4, 7, B, B), BF),
        pltpu.VMEM((3, 2, 4, 7, B, B), BF),
        pltpu.VMEM((2, 2, 4, 256, 256), BF),
        pltpu.VMEM((2, 4, 256, 256), BF),
        pltpu.VMEM((2, 4, 256, 256), BF),
        pltpu.VMEM((2, 3, 256, 256), BF),
        pltpu.VMEM((4, B, 256), F32),
        pltpu.VMEM((2, B, 256), BF),
        pltpu.VMEM((2, B, 256), BF),
        pltpu.VMEM((2, B, 256), BF),
        pltpu.VMEM((2, B, 256), BF),
        dma((2, 4)), dma((2, 4)), dma((NZ,)),
        dma((2, NZ)), dma((3,)),
        dma((2, NZ)), dma((2, NZ)),
        dma((3, 2, 4, NP)), dma((3, 2, 4, NP)),
        dma((3,)), dma((3,)),
        dma((3, 2, 4, NP)), dma((3, 2, 4, NP)),
        dma((2,)), dma((2,)),
        dma((2, 3)), dma((2, 3)),
        dma((2,)), dma((2,)),
        dma((2,)), dma((2,)),
    ]
    acts, grads = pl.pallas_call(
        kernel,
        out_shape=(jax.ShapeDtypeStruct((2, B, 256), BF), jax.ShapeDtypeStruct((21, B, B), BF)),
        in_specs=[anywhere] * 5 + [smem] * 3,
        out_specs=(vmem,) * 2,
        scratch_shapes=scratch,
        compiler_params=pltpu.CompilerParams(
            collective_id=0, has_side_effects=True, vmem_limit_bytes=60 * 2**20
        ),
        cost_estimate=pl.CostEstimate(flops=8_500_000_000, bytes_accessed=6_000_000, transcendentals=229_376),
        name="layer",
    )(x_in, out_grad, gate_tiles, up_tiles, down_tiles, gate_spot, up_spot, down_spot)
    return pl.pallas_call(
        place,
        out_shape=(act, act, tile, tile, tile),
        in_specs=[vmem] * 2,
        out_specs=(anywhere,) * 5,
        scratch_shapes=[dma((5,))],
        name="place",
    )(acts, grads)


def solution(mesh):
    blocks, spots = P(("dp", "feat"), None, None), P(("dp", "feat"))
    return jax.shard_map(
        on_device,
        mesh=mesh,
        in_specs=(P("dp", None),) * 2 + (blocks,) * 3 + (spots,) * 3,
        out_specs=(P("dp", "feat"),) * 2 + (blocks,) * 3,
        check_vma=False,
    )
```
